128 devices in a mesh: blk: 32 (over y_lo, x, z), fsdp: 4 (over y_hi, core).
Axes of the slice: x: 4, y: 4 (y_hi: 2, y_lo: 2; y = y_hi * 2 + y_lo), z: 4, core: 2. Of those that a mesh axis runs over, the one named last changes fastest.
Arguments:
- tokens: bfloat16 [2, 8192, 1024], P(None, ('blk', 'fsdp')), may hold values from -6 to 6
- cotangent: bfloat16 [2, 8192, 1024], P(None, ('blk', 'fsdp')), may hold values from -6 to 6
- w_attn: float32 [4, 1024, 1024], P(None, ('blk', 'fsdp')), as said below
- w_ffn_in: float32 [2, 1024, 2816], P(None, ('blk', 'fsdp')), may hold values from -0.1875 to 0.1875
- w_down: float32 [2816, 1024], P(('blk', 'fsdp')), may hold values from -0.109375 to 0.109375
- gains: float32 [2, 1024], P(None, ('blk', 'fsdp')), may hold values from 0.5 to 1.5
- m_attn: float32 [4, 1024, 1024], P(None, ('blk', 'fsdp')), as said below
- m_ffn_in: float32 [2, 1024, 2816], P(None, ('blk', 'fsdp')), as said below
- m_down: float32 [2816, 1024], P(('blk', 'fsdp')), as said below
- m_gains: float32 [2, 1024], P(None, ('blk', 'fsdp')), as said below
- v_attn: float32 [4, 1024, 1024], P(None, ('blk', 'fsdp')), as said below
- v_ffn_in: float32 [2, 1024, 2816], P(None, ('blk', 'fsdp')), as said below
- v_down: float32 [2816, 1024], P(('blk', 'fsdp')), as said below
- v_gains: float32 [2, 1024], P(None, ('blk', 'fsdp')), as said below
Outputs:
- output: bfloat16 [2, 8192, 1024], P(None, ('blk', 'fsdp'))
- grad_inputs: float32 [2, 8192, 1024], P(None, ('blk', 'fsdp'))
- grad_attn: float32 [4, 1024, 1024], P(None, ('blk', 'fsdp'))
- grad_ffn_in: float32 [2, 1024, 2816], P(None, ('blk', 'fsdp'))
- grad_down: float32 [2816, 1024], P(('blk', 'fsdp'))
- grad_gains: float32 [2, 1024], P(None, ('blk', 'fsdp'))
- new_attn: float32 [4, 1024, 1024], P(None, ('blk', 'fsdp'))
- new_ffn_in: float32 [2, 1024, 2816], P(None, ('blk', 'fsdp'))
- new_down: float32 [2816, 1024], P(('blk', 'fsdp'))
- new_gains: float32 [2, 1024], P(None, ('blk', 'fsdp'))
- second_attn: float32 [4, 1024, 1024], P(None, ('blk', 'fsdp'))
- second_ffn_in: float32 [2, 1024, 2816], P(None, ('blk', 'fsdp'))
- second_down: float32 [2816, 1024], P(('blk', 'fsdp'))
- second_gains: float32 [2, 1024], P(None, ('blk', 'fsdp'))
The draws below stay inside these ranges and needn't reach their ends.
Inputs may be any that keep to these rules, and one draw needn't show every extreme that they name: `w_attn`: independent entries. `m_attn`: independent entries of both signs. `m_ffn_in`: independent entries of both signs. `m_down`: independent entries of both signs. `m_gains`: independent entries of both signs. `v_attn`: positive entries. `v_ffn_in`: positive entries. `v_down`: positive entries. `v_gains`: positive entries.
All inputs are finite; a program needn't handle non-finite values.
Results may differ from the reference program's by a relative error of at most 0.017.
The reference program's roundings to bfloat16 on the way count: a program that leaves them out, or rounds other values in their place, can miss the bound.
Values may be sent and summed in bfloat16 or wider, within the bound.
A program may use at most 384 MiB of HBM per device.

```python
import math
import jax
import jax.numpy as jnp
from jax import lax

D = 1024
HEADS = 16
HEAD = 64
FF = 2816
SEQS = 2
STEP = 10
SEQ_LEN = 8192
TOKENS = 16384


def first_moment(key, extent, factor):
    samples = jnp.clip(jax.random.normal(key, extent, jnp.float32), -4.0, 4.0)
    return samples * (0.11 * factor * math.sqrt(TOKENS))


def second_moment(key, extent, factor):
    levels = jax.random.uniform(key, extent, jnp.float32, math.log(0.5), math.log(2.0))
    return jnp.exp(levels) * (0.002 * factor * factor * TOKENS)


def draw_w_attn(key, part):
    key = jax.random.fold_in(key, 1)
    samples = jnp.clip(jax.random.normal(key, (4, D, D), jnp.float32), -4.0, 4.0)
    scales = jnp.array([(D // 2) ** (-0.5), (D // 2) ** (-0.5), D ** (-0.5), (D // 4) ** (-0.5)], jnp.float32)
    return samples * scales[:, None, None]


def draw_m_attn(key, part):
    key = jax.random.fold_in(key, 2)
    return first_moment(key, (4, D, D), 1.0)


def draw_m_ffn_in(key, part):
    key = jax.random.fold_in(key, 3)
    return first_moment(key, (2, D, FF), 1.0)


def draw_m_down(key, part):
    key = jax.random.fold_in(key, 4)
    return first_moment(key, (FF, D), 0.6)


def draw_m_gains(key, part):
    key = jax.random.fold_in(key, 5)
    return first_moment(key, (2, D), 2.0)


def draw_v_attn(key, part):
    key = jax.random.fold_in(key, 6)
    return second_moment(key, (4, D, D), 1.0)


def draw_v_ffn_in(key, part):
    key = jax.random.fold_in(key, 7)
    return second_moment(key, (2, D, FF), 1.0)


def draw_v_down(key, part):
    key = jax.random.fold_in(key, 8)
    return second_moment(key, (FF, D), 0.6)


def draw_v_gains(key, part):
    key = jax.random.fold_in(key, 9)
    return second_moment(key, (2, D), 2.0)


def level_of(rng, shape, split, smallest, top_value):
    def one(dim, parts):
        steps = jax.random.uniform(jax.random.fold_in(jax.random.fold_in(rng, 6), dim), (parts,), jnp.float32, smallest / len(split), top_value / len(split))
        return jnp.repeat(jnp.exp(steps), shape[dim] // parts).reshape((-1,) + (1,) * (len(shape) - dim - 1))

    loudness = one(*split[0])
    for cut in split[1:]:
        loudness = loudness * one(*cut)
    return loudness


def normal_values(rng, shape, deviation, most, pieces=(), held_as=jnp.bfloat16):
    values = deviation * jax.random.normal(rng, shape, jnp.float32)
    if pieces:
        values = values * level_of(rng, shape, pieces, -0.22, 0.18)
    return jnp.clip(values, -most, most).astype(held_as)


def setup_inputs(seed: int = 0) -> dict:
    key_of = jax.random.split(jax.random.key(seed), 15)
    return {
        "tokens": normal_values(key_of[0], (SEQS, SEQ_LEN, D), 1.0, 6.0, ((1, 128),)),
        "cotangent": normal_values(key_of[1], (SEQS, SEQ_LEN, D), 1.0, 6.0, ((1, 128),)),
        "w_attn": draw_w_attn(jax.random.fold_in(key_of[14], 71), 0),
        "w_ffn_in": normal_values(key_of[3], (2, D, FF), D ** -0.5, 0.1875, ((1, 128),), jnp.float32),
        "w_down": normal_values(key_of[4], (FF, D), FF ** -0.5, 0.109375, ((0, 128),), jnp.float32),
        "gains": jnp.clip(1.0 + 0.1 * jax.random.normal(key_of[5], (2, D), jnp.float32), 0.5, 1.5),
        "m_attn": draw_m_attn(jax.random.fold_in(key_of[14], 71), 0),
        "m_ffn_in": draw_m_ffn_in(jax.random.fold_in(key_of[14], 71), 0),
        "m_down": draw_m_down(jax.random.fold_in(key_of[14], 71), 0),
        "m_gains": draw_m_gains(jax.random.fold_in(key_of[14], 71), 0),
        "v_attn": draw_v_attn(jax.random.fold_in(key_of[14], 71), 0),
        "v_ffn_in": draw_v_ffn_in(jax.random.fold_in(key_of[14], 71), 0),
        "v_down": draw_v_down(jax.random.fold_in(key_of[14], 71), 0),
        "v_gains": draw_v_gains(jax.random.fold_in(key_of[14], 71), 0),
    }


@jax.custom_vjp
def low(v):
    return lax.optimization_barrier(v.astype(jnp.bfloat16)).astype(jnp.float32)

@jax.custom_vjp
def low_back(v):
    return v

def low_keep(v):
    return (low(v), None)

def low_pass(kept, grad):
    return (grad,)

def back_keep(v):
    return (v, None)

def back_low(kept, grad):
    return (low(grad),)
low.defvjp(low_keep, low_pass)
low_back.defvjp(back_keep, back_low)
EPSILON = 1e-05
BETA_ONE = 0.9
BETA_TWO = 0.999
ADAM_EPS = 1e-08

def project(values, weight):
    return jnp.dot(values, weight, precision=lax.Precision.HIGHEST, preferred_element_type=jnp.float32)

def rms_norm(values, gain):
    return values * lax.rsqrt(lax.optimization_barrier(jnp.mean(values * values, axis=-1, keepdims=True)) + EPSILON) * gain

def attend(queries, keys, values):
    length = queries.shape[0]
    blk_rows = min(512, length)
    blocks = length // blk_rows
    score_scale = HEAD ** (-0.5)
    length_bias = math.log(SEQ_LEN)
    key_pos = jnp.arange(length, dtype=jnp.int32)
    grouped = queries.reshape(blocks, blk_rows, HEADS, HEAD)

    def one_block(query_blk, turn_idx):
        logits = jnp.einsum('qhd,khd->hqk', query_blk, keys, precision=lax.Precision.HIGHEST) * score_scale - length_bias
        scores = low_back(logits)
        query_pos = turn_idx * blk_rows + jnp.arange(blk_rows, dtype=jnp.int32)
        visible = query_pos[:, None] >= key_pos[None, :]
        weights = low(jnp.where(visible[None], jax.nn.sigmoid(scores), 0.0))
        return jnp.einsum('hqk,khd->qhd', weights, values, precision=lax.Precision.HIGHEST)
    checked = jax.checkpoint(one_block)
    results = lax.map(lambda pair: checked(pair[0], pair[1]), (grouped, jnp.arange(blocks, dtype=jnp.int32)))
    return results.reshape(length, HEADS * HEAD)

def one_sequence(inputs, attn_low, ffn_low, down_low, gain_low):
    length = inputs.shape[0]
    normed_one = low(rms_norm(inputs, gain_low[0]))
    queries = low_back(low(project(normed_one, attn_low[0])))
    key_rows = low_back(low(project(normed_one, attn_low[1])))
    value_rows = low_back(low(project(normed_one, attn_low[2])))
    attended = attend(queries.reshape(length, HEADS, HEAD), key_rows.reshape(length, HEADS, HEAD), value_rows.reshape(length, HEADS, HEAD))
    attended = low_back(low(attended))
    middle = inputs + low_back(project(attended, attn_low[3]))
    normed_two = low(rms_norm(middle, gain_low[1]))
    gate = low_back(project(normed_two, ffn_low[0]))
    upward = low_back(project(normed_two, ffn_low[1]))
    hidden = low(jax.nn.silu(gate) * upward)
    return middle + project(hidden, down_low)

def adam_step(weight, first, second, grad, rate, decay):
    first_new = BETA_ONE * first + (1.0 - BETA_ONE) * grad
    second_new = BETA_TWO * second + (1.0 - BETA_TWO) * grad * grad
    direction = first_new / (1.0 - BETA_ONE ** STEP) / (jnp.sqrt(second_new / (1.0 - BETA_TWO ** STEP)) + ADAM_EPS)
    return (weight - rate * (direction + decay * weight), second_new)

def reference(tokens, cotangent, w_attn, w_ffn_in, w_down, gains, m_attn, m_ffn_in, m_down, m_gains, v_attn, v_ffn_in, v_down, v_gains):

    def layer(inputs, attn_w, ffn_w, down_w, gain_w):
        attn_low = low(attn_w)
        ffn_low = low(ffn_w)
        down_low = low(down_w)
        gain_low = low(gain_w)

        def scan_step(carry, seq_in):
            return (carry, one_sequence(seq_in, attn_low, ffn_low, down_low, gain_low))
        _, results = lax.scan(scan_step, jnp.zeros((), jnp.float32), inputs)
        return results
    result, pullback = jax.vjp(layer, tokens.astype(jnp.float32), w_attn, w_ffn_in, w_down, gains)
    grad_inputs, grad_attn, grad_ffn, grad_dn, grad_gn = pullback(cotangent.astype(jnp.float32))
    new_attn, second_attn = adam_step(w_attn, m_attn, v_attn, grad_attn, 0.06, 0.1)
    new_ffn, second_ffn = adam_step(w_ffn_in, m_ffn_in, v_ffn_in, grad_ffn, 0.06, 0.1)
    new_dn, second_dn = adam_step(w_down, m_down, v_down, grad_dn, 0.04, 0.1)
    new_gn, second_gn = adam_step(gains, m_gains, v_gains, grad_gn, 0.4, 0.0)
    return (result.astype(jnp.bfloat16), grad_inputs, grad_attn, grad_ffn, grad_dn, grad_gn, new_attn, new_ffn, new_dn, new_gn, second_attn, second_ffn, second_dn, second_gn)
```

```python
import math

import jax
import jax.numpy as jnp
from jax import lax
from jax.experimental import pallas as pl
from jax.experimental.pallas import tpu as pltpu
from jax.sharding import Mesh
from jax.sharding import PartitionSpec as P

HEADS = 16
HEAD = 64
WIDTH = 1024
FF = 2816
HALF = FF // 2
STEP = 10
EPSILON = 1e-05
BETA_ONE = 0.9
BETA_TWO = 0.999
ADAM_EPS = 1e-08
F32 = jnp.float32
BF16 = jnp.bfloat16
AXES = ("yl", "x", "z", "yh", "core")
SWAP = [(0, 1), (1, 0)]
MESH_ID = pl.DeviceIdType.MESH
ORDERS = (("x", "y", "z"), ("y", "z", "x"), ("z", "x", "y"))
PERIODS = 8
TILE = 256
LOG2E = 1.4426950408889634


def coords():
    place = {a: lax.axis_index(a) for a in AXES}
    place["y"] = place["yh"] * 2 + place["yl"]
    return place


def step_id(place, axis, off):
    v = lax.rem(place[axis] + off, 4)
    if axis == "y":
        return {"yl": lax.rem(v, 2), "yh": v // 2}
    return {axis: v}


def region(place, done, axis, v):
    def pick(a):
        return slice(None) if a in done else (v if a == axis else place[a])

    y = pick("y")
    if isinstance(y, slice):
        return (y, pick("x"), pick("z"), y)
    return (lax.rem(y, 2), pick("x"), pick("z"), y // 2)


def halves(cols):
    lo, hi = cols
    mid = lo + ((hi - lo) // 128 + 1) // 2 * 128
    return (lo, mid), (mid, hi)


def split3(width):
    tiles = width // 128
    a = (tiles + 2) // 3
    b = (tiles - a + 1) // 2
    return [(0, a * 128), (a * 128, (a + b) * 128), ((a + b) * 128, width)]


def ring_barrier(place):
    bar = pltpu.get_barrier_semaphore()
    for axis in ("x", "y", "z"):
        for off in (1, 3):
            pl.semaphore_signal(
                bar, inc=1, device_id=step_id(place, axis, off), device_id_type=MESH_ID
            )
    pl.semaphore_wait(bar, 6)


def remote(src, dst, ssem, rsem, i, dev):
    return pltpu.make_async_remote_copy(
        src_ref=src,
        dst_ref=dst,
        send_sem=ssem.at[i],
        recv_sem=rsem.at[i],
        device_id=dev,
        device_id_type=MESH_ID,
    )


def gather_kernel(shard, out, lsem, ssem, rsem):
    place = coords()
    ring_barrier(place)
    parts = split3(shard.shape[-1])
    own = out.at[place["yl"], place["x"], place["z"], place["yh"]]
    local = pltpu.make_async_copy(shard, own, lsem)
    local.start()

    def at(idx, cols):
        return out.at[idx + (slice(None), slice(cols[0], cols[1]))]

    sends = []
    for k in range(3):
        if k == 1:
            local.wait()
        todo = [
            (order[k], order[:k], cols, (k * 3 + p) * 4)
            for p, (order, cols) in enumerate(zip(ORDERS, parts))
        ]
        for axis, done, cols, base in todo:
            me = region(place, done, axis, place[axis])
            src = shard.at[:, cols[0] : cols[1]] if k == 0 else at(me, cols)
            for j, off in enumerate((1, 3)):
                d = remote(src, at(me, cols), ssem, rsem, base + j, step_id(place, axis, off))
                d.start()
                sends.append(d)
        for axis, done, cols, base in todo:
            for j, (off, half) in enumerate(zip((3, 1), halves(cols))):
                got = region(place, done, axis, lax.rem(place[axis] + off, 4))
                r = at(got, cols)
                remote(r, r, ssem, rsem, base + j, step_id(place, axis, off)).wait_recv()
                r = at(got, half)
                d = remote(r, r, ssem, rsem, base + 2 + j, step_id(place, axis, 4 - off))
                d.start()
                sends.append(d)
        for axis, done, cols, base in todo:
            far = region(place, done, axis, lax.rem(place[axis] + 2, 4))
            for j, half in enumerate(halves(cols)):
                r = at(far, half)
                remote(r, r, ssem, rsem, base + 2 + j, step_id(place, axis, 1)).wait_recv()
    for d in sends:
        d.wait_send()


def gather_chips(shard, cid, name):
    return pl.pallas_call(
        gather_kernel,
        out_shape=jax.ShapeDtypeStruct((2, 4, 4, 2) + shard.shape, shard.dtype),
        in_specs=[pl.BlockSpec(memory_space=pl.ANY)],
        out_specs=pl.BlockSpec(memory_space=pl.ANY),
        scratch_shapes=[
            pltpu.SemaphoreType.DMA,
            pltpu.SemaphoreType.DMA((36,)),
            pltpu.SemaphoreType.DMA((36,)),
        ],
        compiler_params=pltpu.CompilerParams(collective_id=cid, has_side_effects=True),
        name=name,
    )(shard).reshape(64 * shard.shape[0], shard.shape[1])


def lead(place, done, axis, v):
    return region(place, done, axis, v)


def scatter_kernel(grads, out, *rest):
    place = coords()
    parts = split3(grads.shape[-1])
    work = rest[0:3]
    bufs = rest[3:12]
    lsem, ssem, rsem = rest[12:]
    loads = []
    for p, cols in enumerate(parts):
        d = pltpu.make_async_copy(
            grads.at[:, :, :, :, :, cols[0] : cols[1]], work[p], lsem.at[p]
        )
        d.start()
        loads.append(d)
    ring_barrier(place)
    sends = []
    for k in range(3):
        todo = []
        for p, (order, cols) in enumerate(zip(ORDERS, parts)):
            back = order[::-1]
            axis, left = back[k], back[k + 1 :]
            todo.append((p, axis, left, halves((0, cols[1] - cols[0])), (k * 3 + p) * 4))
        if k == 0:
            for d in loads:
                d.wait()

        def dims(left):
            return tuple(
                n
                for n, a in zip((2, 4, 4, 2), ("y", "x", "z", "y"))
                if a in left
            )

        def chunk(p, left, axis, off, cols):
            idx = region(place, left, axis, lax.rem(place[axis] + off, 4))
            return work[p].at[idx + (slice(None), slice(cols[0], cols[1]))]

        def buf(p, k, j, cols):
            b = bufs[p * 3 + k]
            return b.at[(j,) + (slice(None),) * (len(b.shape) - 2) + (slice(cols[0], cols[1]),)]

        for p, axis, left, hv, base in todo:
            for j, off in enumerate((1, 3)):
                d = remote(
                    chunk(p, left, axis, 2, hv[j]),
                    buf(p, k, j, hv[j]),
                    ssem,
                    rsem,
                    base + j,
                    step_id(place, axis, off),
                )
                d.start()
                sends.append(d)
        for p, axis, left, hv, base in todo:
            whole = (0, hv[1][1])
            for j, off in enumerate((1, 3)):
                r = buf(p, k, j, hv[j])
                remote(r, r, ssem, rsem, base + j, step_id(place, axis, 4 - off)).wait_recv()
                add_into(chunk(p, left, axis, off, hv[j]), [r])
                d = remote(
                    chunk(p, left, axis, off, whole),
                    buf(p, k, j + 2, whole),
                    ssem,
                    rsem,
                    base + 2 + j,
                    step_id(place, axis, off),
                )
                d.start()
                sends.append(d)
        for p, axis, left, hv, base in todo:
            whole = (0, hv[1][1])
            got = []
            for j, off in enumerate((1, 3)):
                r = buf(p, k, j + 2, whole)
                remote(r, r, ssem, rsem, base + 2 + j, step_id(place, axis, 4 - off)).wait_recv()
                got.append(r)
            if k < 2:
                add_into(chunk(p, left, axis, 0, whole), got)
            else:
                total = chunk(p, left, axis, 0, whole)[...].astype(F32)
                for r in got:
                    total = total + r[...].astype(F32)
                out[:, parts[p][0] : parts[p][1]] = total
    for d in sends:
        d.wait_send()


def add_into(target, terms):
    dims = target.shape[:-2]
    count = math.prod(dims)

    def one(i, _):
        idx = []
        for n in reversed(dims):
            idx.append(lax.rem(i, n))
            i = i // n
        idx = tuple(reversed(idx))
        total = target[idx].astype(F32)
        for t in terms:
            total = total + t[idx].astype(F32)
        target[idx] = total.astype(BF16)
        return 0

    lax.fori_loop(0, count, one, 0)


def scatter_chips(grads, cid, name):
    width = grads.shape[-1]
    parts = split3(width)
    size = {"y": (2, 2), "x": (4,), "z": (4,)}
    scratch = [pltpu.VMEM((2, 4, 4, 2, 16, hi - lo), BF16) for lo, hi in parts]
    for order, (lo, hi) in zip(ORDERS, parts):
        back = order[::-1]
        for k in range(3):
            left = back[k + 1 :]
            dims = tuple(
                n for n, a in zip((2, 4, 4, 2), ("y", "x", "z", "y")) if a in left
            )
            scratch.append(pltpu.VMEM((4,) + dims + (16, hi - lo), BF16))
    scratch += [
        pltpu.SemaphoreType.DMA((3,)),
        pltpu.SemaphoreType.DMA((36,)),
        pltpu.SemaphoreType.DMA((36,)),
    ]
    return pl.pallas_call(
        scatter_kernel,
        out_shape=jax.ShapeDtypeStruct((16, width), F32),
        in_specs=[pl.BlockSpec(memory_space=pl.ANY)],
        out_specs=pl.BlockSpec(memory_space=pltpu.VMEM),
        scratch_shapes=scratch,
        compiler_params=pltpu.CompilerParams(
            collective_id=cid, has_side_effects=True, vmem_limit_bytes=56 * 1024 * 1024
        ),
        name=name,
    )(grads.reshape(2, 4, 4, 2, 16, width))


def dot_nt(a, b):
    return lax.dot_general(a, b, (((1,), (1,)), ((), ())), preferred_element_type=F32)


def dot_nn(a, b):
    return lax.dot_general(a, b, (((1,), (0,)), ((), ())), preferred_element_type=F32)


def sigmoid_of(raw):
    return 1.0 / (1.0 + jnp.exp2(raw * (-LOG2E / 8.0) + 13.0))


def z_barrier(place):
    bar = pltpu.get_barrier_semaphore()
    for off in (1, 2, 3):
        pl.semaphore_signal(bar, inc=1, device_id=step_id(place, "z", off), device_id_type=MESH_ID)
    pl.semaphore_wait(bar, 3)


def attend_kernel(qkv, kv_all, att, acc, ssem, rsem):
    place = coords()
    z = place["z"]
    z_barrier(place)

    def rows(p):
        return pl.ds(pl.multiple_of(p * TILE, TILE), TILE)

    def piece(p, j, off):
        return remote(
            qkv.at[rows(p), 128:256],
            kv_all.at[z, rows(p)],
            ssem,
            rsem,
            p * 3 + j,
            step_id(place, "z", off),
        )

    def start(p, _):
        for j, off in enumerate((1, 3, 2)):
            piece(p, j, off).start()
        return 0

    lax.fori_loop(0, PERIODS, start, 0)
    kv_all[z] = qkv[:, 128:256]

    def tile(p, _):
        for j, off in enumerate((3, 1, 2)):
            r = kv_all.at[lax.rem(z + off, 4), rows(p)]
            remote(r, r, ssem, rsem, p * 3 + j, step_id(place, "z", off)).wait_recv()
        q = qkv[rows(p), 0:128]
        acc[...] = jnp.zeros_like(acc)

        def earlier(r, _):
            total = acc[...]
            for zz in range(4):
                kv = kv_all[zz, rows(r)]
                total = total + dot_nn(sigmoid_of(dot_nt(q, kv)).astype(BF16), kv)
            acc[...] = total
            return 0

        lax.fori_loop(0, p, earlier, 0)
        total = acc[...]
        q_pos = z * TILE + lax.broadcasted_iota(jnp.int32, (TILE, TILE), 0)
        k_pos = lax.broadcasted_iota(jnp.int32, (TILE, TILE), 1)
        for zz in range(4):
            kv = kv_all[zz, rows(p)]
            w = jnp.where(q_pos >= k_pos + zz * TILE, sigmoid_of(dot_nt(q, kv)), 0.0)
            total = total + dot_nn(w.astype(BF16), kv)
        att[rows(p), :] = total.astype(BF16)
        return 0

    lax.fori_loop(0, PERIODS, tile, 0)

    def end(p, _):
        for j, off in enumerate((1, 3, 2)):
            piece(p, j, off).wait_send()
        return 0

    lax.fori_loop(0, PERIODS, end, 0)


def attend(qkv, cid):
    n = qkv.shape[0]
    return pl.pallas_call(
        attend_kernel,
        out_shape=(
            jax.ShapeDtypeStruct((4, n, 128), BF16),
            jax.ShapeDtypeStruct((n, 128), BF16),
        ),
        in_specs=[pl.BlockSpec(memory_space=pltpu.VMEM)],
        out_specs=[pl.BlockSpec(memory_space=pltpu.VMEM)] * 2,
        scratch_shapes=[
            pltpu.VMEM((TILE, 128), F32),
            pltpu.SemaphoreType.DMA((24,)),
            pltpu.SemaphoreType.DMA((24,)),
        ],
        compiler_params=pltpu.CompilerParams(
            collective_id=cid, has_side_effects=True, vmem_limit_bytes=48 * 1024 * 1024
        ),
        name="attend",
    )(qkv)


def attend_back_kernel(qkv, kv_all, da_all, out, kvt, acc, dqt, own, stage, got, ssem, rsem):
    place = coords()
    z = place["z"]
    z_barrier(place)
    dqt[...] = jnp.zeros_like(dqt)

    def rows(p):
        return pl.ds(pl.multiple_of(p * TILE, TILE), TILE)

    def piece(r, j, off):
        return remote(
            stage.at[lax.rem(z + off, 4), rows(r)],
            got.at[j, rows(r)],
            ssem,
            rsem,
            r * 3 + j,
            step_id(place, "z", off),
        )

    def keys(r, _):
        for zz in range(4):
            kvt[zz] = jnp.transpose(kv_all[zz, rows(r)].astype(F32)).astype(BF16)
        acc[...] = jnp.zeros_like(acc)

        def block(p, masked):
            q = qkv[rows(p), 0:128]
            da = da_all[rows(p), :]
            dq = dqt[:, rows(p)]
            if masked:
                q_pos = z * TILE + lax.broadcasted_iota(jnp.int32, (TILE, TILE), 1)
                k_pos = lax.broadcasted_iota(jnp.int32, (TILE, TILE), 0)
            for zz in range(4):
                kv = kv_all[zz, rows(r)]
                sg = sigmoid_of(dot_nt(kv, q))
                if masked:
                    sg = jnp.where(q_pos >= k_pos + zz * TILE, sg, 0.0)
                ds = (dot_nt(kv, da) * (sg * (1.0 - sg))).astype(BF16)
                acc[zz] += dot_nn(ds, q) + dot_nn(sg.astype(BF16), da)
                dq = dq + dot_nn(kvt[zz], ds)
            dqt[:, rows(p)] = dq

        block(r, True)

        def later(p, _):
            block(p, False)
            return 0

        lax.fori_loop(r + 1, PERIODS, later, 0)
        for zz in range(4):
            stage[zz, rows(r)] = acc[zz].astype(BF16)
        own[rows(r), :] = acc[z]
        for j, off in enumerate((1, 3, 2)):
            piece(r, j, off).start()
        return 0

    lax.fori_loop(0, PERIODS, keys, 0)
    scale = jnp.where(lax.broadcasted_iota(jnp.int32, (TILE, 128), 1) < HEAD, 0.125, 1.0)

    def finish(p, _):
        total = own[rows(p), :]
        for j, off in enumerate((1, 3, 2)):
            piece(p, j, off).wait()
            total = total + got[j, rows(p)].astype(F32)
        out[rows(p), 128:256] = (total * scale).astype(BF16)
        out[rows(p), 0:128] = (jnp.transpose(dqt[:, rows(p)]) * 0.125).astype(BF16)
        return 0

    lax.fori_loop(0, PERIODS, finish, 0)


def attend_back(qkv, kv_all, da, cid):
    n = qkv.shape[0]
    return pl.pallas_call(
        attend_back_kernel,
        out_shape=jax.ShapeDtypeStruct((n, 256), BF16),
        in_specs=[pl.BlockSpec(memory_space=pltpu.VMEM)] * 3,
        out_specs=pl.BlockSpec(memory_space=pltpu.VMEM),
        scratch_shapes=[
            pltpu.VMEM((4, 128, TILE), BF16),
            pltpu.VMEM((4, TILE, 128), F32),
            pltpu.VMEM((128, n), F32),
            pltpu.VMEM((n, 128), F32),
            pltpu.VMEM((4, n, 128), BF16),
            pltpu.VMEM((3, n, 128), BF16),
            pltpu.SemaphoreType.DMA((24,)),
            pltpu.SemaphoreType.DMA((24,)),
        ],
        compiler_params=pltpu.CompilerParams(
            collective_id=cid, has_side_effects=True, vmem_limit_bytes=48 * 1024 * 1024
        ),
        name="attend_back",
    )(qkv, kv_all, da)


def normalize(values):
    inverse = lax.rsqrt(jnp.mean(values * values, axis=-1, keepdims=True) + EPSILON)
    return (values * inverse, inverse)


def norm_back(grad_hat, scaled, inverse):
    return inverse * (grad_hat - scaled * jnp.mean(grad_hat * scaled, axis=-1, keepdims=True))


def outer_sum(left, right):
    return lax.dot_general(left, right, (((0,), (0,)), ((), ())), preferred_element_type=F32)


def adam_step(weight, first, second, grad, rate, decay):
    first_new = BETA_ONE * first + (1.0 - BETA_ONE) * grad
    second_new = BETA_TWO * second + (1.0 - BETA_TWO) * grad * grad
    direction = (
        first_new
        / (1.0 - BETA_ONE**STEP)
        / (jnp.sqrt(second_new / (1.0 - BETA_TWO**STEP)) + ADAM_EPS)
    )
    return (weight - rate * (direction + decay * weight), second_new)


def other_core(values):
    return lax.ppermute(values, "core", SWAP)


def both(core, values, axis):
    other = other_core(values)
    first = jnp.where(core == 0, values, other)
    last = jnp.where(core == 0, other, values)
    return jnp.concatenate([first, last], axis=axis)


def by_core(values):
    cut = values.reshape(values.shape[0], 64, 2, 22)
    main = jnp.moveaxis(cut[..., :16], 2, 0).reshape(2, values.shape[0], 1024)
    tail = jnp.moveaxis(cut[..., 16:], 2, 0).reshape(2, values.shape[0], 384)
    return jnp.concatenate([main, tail], axis=-1)


def from_cores(values):
    n = values.shape[1]
    main = jnp.moveaxis(values[..., :1024].reshape(2, n, 64, 16), 0, 2)
    tail = jnp.moveaxis(values[..., 1024:].reshape(2, n, 64, 6), 0, 2)
    return jnp.concatenate([main, tail], axis=-1).reshape(n, FF)


def pick(values, core):
    return lax.dynamic_index_in_dim(values, core, 0, keepdims=False)


def spread(offset):
    src = lax.broadcasted_iota(jnp.int32, (512, 1024), 0)
    dst = lax.broadcasted_iota(jnp.int32, (512, 1024), 1)
    return (dst == src // HEAD * 128 + src % HEAD + offset).astype(BF16)


def to_heads(values):
    n = values.shape[-1] // 8
    return values.reshape(2, 128, 8, n).transpose(0, 2, 1, 3).reshape(2048, n)


def from_heads(values):
    n = values.shape[-1]
    return values.reshape(2, 8, 128, n).transpose(0, 2, 1, 3).reshape(256, 8 * n)


def exchange(values):
    return lax.all_to_all(values, ("yl", "x", "yh"), 0, 0, tiled=True)


def dot(a, b):
    return jnp.dot(a, b, preferred_element_type=F32)


def body(
    tokens, cotangent, w_attn, w_ffn_in, w_down, gains, m_attn, m_ffn_in, m_down, m_gains,
    v_attn, v_ffn_in, v_down, v_gains,
):
    core = lax.axis_index("core")
    attn_low = w_attn.astype(BF16)
    ffn_low = w_ffn_in.astype(BF16)
    down_low = w_down.astype(BF16)
    qkv_low = attn_low[:3].reshape(3, 8, 2, 8, HEAD)
    key_value = jnp.stack([qkv_low[1], qkv_low[2]], axis=3)
    early = jnp.concatenate(
        [
            qkv_low[0].transpose(1, 0, 2, 3).reshape(2, 8, 512),
            key_value.transpose(1, 0, 2, 3, 4).reshape(2, 8, 1024),
        ],
        axis=-1,
    )
    late = jnp.concatenate([by_core(ffn_low[0]), by_core(ffn_low[1])], axis=-1)
    packed = jnp.concatenate([early, late], axis=-1)
    mine = pick(packed, core)
    theirs = other_core(pick(packed, 1 - core))
    rows16 = jnp.concatenate(
        [jnp.where(core == 0, mine, theirs), jnp.where(core == 0, theirs, mine)], axis=0
    )
    out_gain = jnp.concatenate(
        [
            attn_low[3],
            jnp.pad(gains.astype(BF16).T, ((0, 0), (0, 126))),
        ],
        axis=-1,
    )
    out_gain = both(core, out_gain, 0)
    shard_one = jnp.concatenate([rows16[:, :1536], out_gain[:, 1024:]], axis=-1)
    shard_two = jnp.concatenate(
        [rows16[:, 1536:], out_gain[:, :1024], down_low[:16], down_low[16:].reshape(16, 384)],
        axis=-1,
    )
    full_one = gather_chips(shard_one, 1, "gather_early")
    full_two = gather_chips(shard_two, 2, "gather_late")
    w_q = full_one[:, :512]
    w_kv = full_one[:, 512:1536]
    gain_one = full_one[:, 1536].astype(F32)
    gain_two = full_one[:, 1537].astype(F32)
    w_gate = full_two[:, :HALF]
    w_up = full_two[:, HALF : 2 * HALF]
    w_out = full_two[:, 2 * HALF : 2 * HALF + 1024]
    w_dn = jnp.concatenate(
        [
            full_two[:, 2 * HALF + 1024 : 2 * HALF + 2048],
            full_two[:, 2 * HALF + 2048 :].reshape(384, 1024),
        ],
        axis=0,
    )
    inputs = both(core, tokens, 1).astype(F32).reshape(256, WIDTH)
    grad_rows = both(core, cotangent, 1).reshape(256, WIDTH)

    scaled_one, inverse_one = normalize(inputs)
    normed_one = (scaled_one * gain_one).astype(BF16)
    queries = dot(dot(normed_one, w_q).astype(BF16), spread(0)).astype(BF16)
    keys_values = dot(normed_one, w_kv).astype(BF16)
    qkv = exchange(jnp.concatenate([to_heads(queries), to_heads(keys_values)], axis=-1))
    kv_all, att = attend(qkv, 3)
    att = from_heads(exchange(att))
    att_half = lax.dot_general(
        att, spread(HEAD), (((1,), (1,)), ((), ())), preferred_element_type=F32
    ).astype(BF16)
    attn_out = both(core, att_half, 1)
    middle = inputs + dot(attn_out, w_out)
    scaled_two, inverse_two = normalize(middle)
    normed_two = (scaled_two * gain_two).astype(BF16)
    gate = dot(normed_two, w_gate)
    upward = dot(normed_two, w_up)
    hidden = (jax.nn.silu(gate) * upward).astype(BF16)
    result_part = dot(hidden, w_dn).reshape(2, 2, 64, WIDTH)
    mid_own = pick(middle.reshape(2, 2, 64, WIDTH).swapaxes(0, 1), core)
    part_own = pick(result_part.swapaxes(0, 1), core)
    part_other = other_core(pick(result_part.swapaxes(0, 1), 1 - core))
    output = (mid_own + (part_own + part_other)).astype(BF16)

    grad_dn = outer_sum(hidden, grad_rows)
    grad_hidden = dot_nt(grad_rows, w_dn)
    squash = jax.nn.sigmoid(gate)
    grad_up = (grad_hidden * jax.nn.silu(gate)).astype(BF16)
    grad_gate = (grad_hidden * upward * (squash + gate * squash * (1.0 - squash))).astype(BF16)
    grad_normed_two = dot_nt(grad_gate, w_gate) + dot_nt(grad_up, w_up)
    grad_normed_two = grad_normed_two + other_core(grad_normed_two)
    gain_grad_two = jnp.sum(grad_normed_two * scaled_two, axis=0)
    grad_middle = grad_rows.astype(F32) + norm_back(
        grad_normed_two * gain_two, scaled_two, inverse_two
    )
    branch_grad = grad_middle.astype(BF16)
    w_out_half = lax.dynamic_slice_in_dim(w_out, core * 512, 512, 0)
    grad_att = dot_nt(branch_grad, w_out_half).astype(BF16)
    grad_att = exchange(to_heads(dot(grad_att, spread(HEAD)).astype(BF16)))
    grad_qkv = exchange(attend_back(qkv, kv_all, grad_att, 4))
    grad_q = lax.dot_general(
        from_heads(grad_qkv[:, :128]),
        spread(0),
        (((1,), (1,)), ((), ())),
        preferred_element_type=F32,
    ).astype(BF16)
    grad_kv = from_heads(grad_qkv[:, 128:])
    grad_normed_one = dot_nt(grad_q, w_q) + dot_nt(grad_kv, w_kv)
    grad_normed_one = grad_normed_one + other_core(grad_normed_one)
    gain_grad_one = jnp.sum(grad_normed_one * scaled_one, axis=0)
    grad_inputs = grad_middle + norm_back(grad_normed_one * gain_one, scaled_one, inverse_one)
    grad_inputs = pick(grad_inputs.reshape(2, 2, 64, WIDTH).swapaxes(0, 1), core)

    branch_half = lax.dynamic_slice_in_dim(branch_grad, core * 512, 512, 1)
    lanes = lax.broadcasted_iota(jnp.int32, (1024, 128), 1)
    gain_cols = jnp.where(lanes == 0, gain_grad_one[:, None], gain_grad_two[:, None])
    grads_two = jnp.concatenate(
        [
            outer_sum(normed_two, grad_gate).astype(BF16),
            outer_sum(normed_two, grad_up).astype(BF16),
            outer_sum(attn_out, branch_half).astype(BF16),
            grad_dn[:1024].astype(BF16),
            grad_dn[1024:].astype(BF16).reshape(1024, 384),
        ],
        axis=-1,
    )
    grads_one = jnp.concatenate(
        [
            outer_sum(normed_one, grad_q).astype(BF16),
            outer_sum(normed_one, grad_kv).astype(BF16),
            gain_cols.astype(BF16),
        ],
        axis=-1,
    )
    sum_two = scatter_chips(grads_two, 5, "scatter_ffn")
    sum_one = scatter_chips(grads_one, 6, "scatter_attn")

    wide = 2 * HALF + 512
    rows = jnp.concatenate([sum_two[:, :wide], sum_one[:, :1536]], axis=-1).reshape(2, 8, wide + 1536)
    mine = pick(rows, core)
    theirs = other_core(pick(rows, 1 - core))
    pair = jnp.stack([jnp.where(core == 0, mine, theirs), jnp.where(core == 0, theirs, mine)])
    ffn_part = jnp.stack([from_cores(pair[..., :HALF]), from_cores(pair[..., HALF : 2 * HALF])])
    out_part = jnp.concatenate([pair[0, :, 2 * HALF : wide], pair[1, :, 2 * HALF : wide]], axis=-1)
    q_part = pair[..., wide : wide + 512].transpose(1, 0, 2).reshape(8, 1024)
    kv_part = pair[..., wide + 512 :].reshape(2, 8, 8, 2, HEAD).transpose(3, 1, 0, 2, 4).reshape(2, 8, 1024)
    attn_part = jnp.concatenate([q_part[None], kv_part, out_part[None]], axis=0)
    down_part = jnp.concatenate(
        [sum_two[:, wide : wide + 1024], sum_two[:, wide + 1024 :].reshape(6, 1024)], axis=0
    )
    gain_part = pick(sum_one[:, 1536:1538].reshape(2, 8, 2), core).T

    new_attn, second_attn = adam_step(w_attn, m_attn, v_attn, attn_part, 0.06, 0.1)
    new_ffn, second_ffn = adam_step(w_ffn_in, m_ffn_in, v_ffn_in, ffn_part, 0.06, 0.1)
    new_dn, second_dn = adam_step(w_down, m_down, v_down, down_part, 0.04, 0.1)
    new_gn, second_gn = adam_step(gains, m_gains, v_gains, gain_part, 0.4, 0.0)
    return (
        output, grad_inputs, attn_part, ffn_part, down_part, gain_part,
        new_attn, new_ffn, new_dn, new_gn, second_attn, second_ffn, second_dn, second_gn,
    )


def solution(mesh):
    fine = Mesh(mesh.devices.reshape(2, 4, 4, 2, 2), AXES)
    rows3 = P(None, AXES, None)
    rows2 = P(AXES, None)
    cols = P(None, AXES)
    weights = (rows3, rows3, rows2, cols)
    return jax.shard_map(
        body,
        mesh=fine,
        in_specs=(rows3, rows3) + weights * 3,
        out_specs=(rows3, rows3) + weights * 3,
        check_vma=False,
    )
```

```python
import math

import jax
import jax.numpy as jnp
from jax import lax
from jax.experimental import pallas as pl
from jax.experimental.pallas import tpu as pltpu
from jax.sharding import Mesh
from jax.sharding import PartitionSpec as P

HEADS = 16
HEAD = 64
WIDTH = 1024
FF = 2816
HALF = FF // 2
STEP = 10
EPSILON = 1e-05
BETA_ONE = 0.9
BETA_TWO = 0.999
ADAM_EPS = 1e-08
F32 = jnp.float32
BF16 = jnp.bfloat16
AXES = ("yl", "x", "z", "yh", "core")
SWAP = [(0, 1), (1, 0)]
MESH_ID = pl.DeviceIdType.MESH
ORDERS = (("x", "y", "z"), ("y", "z", "x"), ("z", "x", "y"))
PERIODS = 8
TILE = 256
LOG2E = 1.4426950408889634


def coords():
    place = {a: lax.axis_index(a) for a in AXES}
    place["y"] = place["yh"] * 2 + place["yl"]
    return place


def step_id(place, axis, off):
    v = lax.rem(place[axis] + off, 4)
    if axis == "y":
        return {"yl": lax.rem(v, 2), "yh": v // 2}
    return {axis: v}


def region(place, done, axis, v):
    def pick(a):
        return slice(None) if a in done else (v if a == axis else place[a])

    y = pick("y")
    if isinstance(y, slice):
        return (y, pick("x"), pick("z"), y)
    return (lax.rem(y, 2), pick("x"), pick("z"), y // 2)


def halves(cols):
    lo, hi = cols
    mid = lo + ((hi - lo) // 128 + 1) // 2 * 128
    return (lo, mid), (mid, hi)


def split3(width):
    tiles = width // 128
    a = max(2, tiles // 4) if tiles > 20 else (tiles + 1) // 3
    b = (tiles - a + 1) // 2
    return [(0, a * 128), (a * 128, (a + b) * 128), ((a + b) * 128, width)]


def greet(place, pairs):
    bar = pltpu.get_barrier_semaphore()
    for axis, off in pairs:
        pl.semaphore_signal(
            bar, inc=1, device_id=step_id(place, axis, off), device_id_type=MESH_ID
        )
    pl.semaphore_wait(bar, len(pairs))


def remote(src, dst, ssem, rsem, i, dev):
    return pltpu.make_async_remote_copy(
        src_ref=src,
        dst_ref=dst,
        send_sem=ssem.at[i],
        recv_sem=rsem.at[i],
        device_id=dev,
        device_id_type=MESH_ID,
    )


NEAR = [(a, o) for a in ("x", "y", "z") for o in (1, 3)]
EVERY = [(a, o) for a in ("x", "y", "z") for o in (1, 3, 2)]


class Gather:
    def __init__(self, place, shard, out, ssem, rsem, base):
        self.place, self.shard, self.out = place, shard, out
        self.ssem, self.rsem, self.base = ssem, rsem, base
        self.parts = list(zip(ORDERS, split3(out.shape[-1])))
        self.sends = []

    def at(self, idx, cols):
        return self.out.at[idx + (slice(None), slice(cols[0], cols[1]))]

    def copy(self, src, dst, i, axis, off):
        return remote(
            src, dst, self.ssem, self.rsem, self.base + i, step_id(self.place, axis, off)
        )

    def where(self, k, order, off):
        return region(self.place, order[:k], order[k], lax.rem(self.place[order[k]] + off, 4))

    def send(self, k):
        for p, (order, cols) in enumerate(self.parts):
            dst = self.at(self.where(k, order, 0), cols)
            src = self.shard.at[:, cols[0] : cols[1]] if k == 0 else dst
            for j, off in enumerate((1, 3, 2) if k < 2 else (1, 3)):
                d = self.copy(src, dst, k * 9 + p * 3 + j, order[k], off)
                d.start()
                self.sends.append(d)

    def receive(self, k):
        for p, (order, cols) in enumerate(self.parts):
            for j, off in enumerate((3, 1, 2)):
                r = self.at(self.where(k, order, off), cols)
                self.copy(r, r, k * 9 + p * 3 + j, order[k], off).wait_recv()

    def forward(self):
        for p, (order, cols) in enumerate(self.parts):
            for j, (off, half) in enumerate(zip((3, 1), halves(cols))):
                idx = self.where(2, order, off)
                r = self.at(idx, cols)
                self.copy(r, r, 18 + p * 3 + j, order[2], off).wait_recv()
                r = self.at(idx, half)
                d = self.copy(r, r, 27 + p * 2 + j, order[2], 4 - off)
                d.start()
                self.sends.append(d)

    def last(self):
        for p, (order, cols) in enumerate(self.parts):
            far = self.where(2, order, 2)
            for j, half in enumerate(halves(cols)):
                r = self.at(far, half)
                self.copy(r, r, 27 + p * 2 + j, order[2], 1).wait_recv()

    def finish(self):
        for d in self.sends:
            d.wait_send()
        self.sends = []


GATHER_SEMS = 33


def gather_kernel(one, two, out_one, out_two, lsem, ssem, rsem):
    place = coords()
    locals_ = []
    for i, (shard, out) in enumerate(((one, out_one), (two, out_two))):
        own = out.at[place["yl"], place["x"], place["z"], place["yh"]]
        d = pltpu.make_async_copy(shard, own, lsem.at[i])
        d.start()
        locals_.append(d)
    greet(place, EVERY)
    a = Gather(place, one, out_one, ssem, rsem, 0)
    b = Gather(place, two, out_two, ssem, rsem, GATHER_SEMS)
    a.send(0)
    b.send(0)
    for d in locals_:
        d.wait()
    a.receive(0)
    a.send(1)
    b.receive(0)
    a.receive(1)
    a.send(2)
    b.send(1)
    a.forward()
    a.last()
    b.receive(1)
    a.finish()
    b.finish()


def gather_chips(one, two, cid):
    return pl.pallas_call(
        gather_kernel,
        out_shape=tuple(
            jax.ShapeDtypeStruct((2, 4, 4, 2) + s.shape, s.dtype) for s in (one, two)
        ),
        in_specs=[pl.BlockSpec(memory_space=pl.ANY)] * 2,
        out_specs=[pl.BlockSpec(memory_space=pl.ANY)] * 2,
        scratch_shapes=[
            pltpu.SemaphoreType.DMA((2,)),
            pltpu.SemaphoreType.DMA((2 * GATHER_SEMS,)),
            pltpu.SemaphoreType.DMA((2 * GATHER_SEMS,)),
        ],
        compiler_params=pltpu.CompilerParams(collective_id=cid, has_side_effects=True),
        name="gather",
    )(one, two)


def part_dims(left):
    return tuple(n for n, a in zip((2, 4, 4, 2), ("y", "x", "z", "y")) if a in left)


def part_shapes(width, k):
    return [
        part_dims(order[::-1][k:]) + (16, hi - lo)
        for order, (lo, hi) in zip(ORDERS, split3(width))
    ]


def sum_blocks(target, terms):
    dims = target.shape[:-2]

    def one(i, _):
        idx = []
        for n in reversed(dims):
            idx.append(lax.rem(i, n))
            i = i // n
        idx = tuple(reversed(idx))
        total = terms[0][idx].astype(F32)
        for t in terms[1:]:
            total = total + t[idx].astype(F32)
        target[idx] = total.astype(target.dtype)
        return 0

    if dims:
        lax.fori_loop(0, math.prod(dims), one, 0)
    else:
        one(0, 0)


class Scatter:
    def __init__(self, place, views, ssem, rsem, base):
        self.place, self.views = place, views
        self.ssem, self.rsem, self.base = ssem, rsem, base
        self.sends = []

    def copy(self, src, dst, i, axis, off):
        return remote(
            src, dst, self.ssem, self.rsem, self.base + i, step_id(self.place, axis, off)
        )

    def chunk(self, p, k, off, cols=None):
        back = ORDERS[p][::-1]
        idx = region(
            self.place, back[k + 1 :], back[k], lax.rem(self.place[back[k]] + off, 4)
        )
        if k > 0:
            gone = back[:k]
            idx = tuple(
                i for i, a in zip(idx, ("y", "x", "z", "y")) if a not in gone
            )
        view = self.views[p]
        lo, hi = cols or (0, view.shape[-1])
        return view.at[idx + (slice(None), slice(lo, hi))]

    def cut(self, p):
        return halves((0, self.views[p].shape[-1]))

    def wide_send(self, far):
        for p in range(3):
            axis = ORDERS[p][2]
            for j, (off, half) in enumerate(zip((1, 3), self.cut(p))):
                d = self.copy(self.chunk(p, 0, 2, half), far[p][j], p * 4 + j, axis, off)
                d.start()
                self.sends.append(d)

    def wide_forward(self, far, near):
        for p in range(3):
            axis = ORDERS[p][2]
            cut = self.cut(p)
            for j, off in enumerate((1, 3)):
                got = far[p][j]
                self.copy(got, got, p * 4 + j, axis, 4 - off).wait_recv()
                sum_blocks(got, [got, self.chunk(p, 0, off, cut[j])])
                for i, src in ((j, got), (1 - j, self.chunk(p, 0, off, cut[1 - j]))):
                    lo, hi = cut[i]
                    n = len(near[p].shape) - 2
                    dst = near[p].at[(j,) + (slice(None),) * n + (slice(lo, hi),)]
                    d = self.copy(src, dst, 12 + p * 4 + j * 2 + (i != j), axis, off)
                    d.start()
                    self.sends.append(d)

    def wide_last(self, near, out):
        for p in range(3):
            axis = ORDERS[p][2]
            cut = self.cut(p)
            n = len(near[p].shape) - 2
            for j, off in enumerate((1, 3)):
                for i in (j, 1 - j):
                    lo, hi = cut[i]
                    dst = near[p].at[(j,) + (slice(None),) * n + (slice(lo, hi),)]
                    self.copy(dst, dst, 12 + p * 4 + j * 2 + (i != j), axis, 4 - off).wait_recv()
            sum_blocks(out[p], [self.chunk(p, 0, 0), near[p].at[0], near[p].at[1]])
        self.finish()
        self.views = out

    def send(self, k, bufs):
        for p in range(3):
            axis = ORDERS[p][2 - k]
            for j, off in enumerate((1, 3, 2)):
                i = 24 + (k - 1) * 9 + p * 3 + j
                d = self.copy(self.chunk(p, k, off), bufs[p].at[j], i, axis, off)
                d.start()
                self.sends.append(d)

    def receive(self, k, bufs, out):
        for p in range(3):
            axis = ORDERS[p][2 - k]
            for j, off in enumerate((1, 3, 2)):
                r = bufs[p].at[j]
                self.copy(r, r, 24 + (k - 1) * 9 + p * 3 + j, axis, 4 - off).wait_recv()
            sum_blocks(out[p], [self.chunk(p, k, 0)] + [bufs[p].at[j] for j in range(3)])
        self.finish()
        self.views = out

    def finish(self):
        for d in self.sends:
            d.wait_send()
        self.sends = []


SCATTER_SEMS = 42


def wide_scratch(width):
    far, near = [], []
    for shape in part_shapes(width, 1):
        for lo, hi in halves((0, shape[-1])):
            far.append(pltpu.VMEM(shape[:-1] + (hi - lo,), BF16))
        near.append(pltpu.VMEM((2,) + shape, BF16))
    return far + near


def narrow_scratch(width, k):
    return [pltpu.VMEM((3,) + shape, BF16) for shape in part_shapes(width, k + 1)]


def wide_bufs(refs):
    return [refs[2 * p : 2 * p + 2] for p in range(3)], refs[6:9]


def column_views(ref):
    whole = (slice(None),) * (len(ref.shape) - 1)
    return [ref.at[whole + (slice(lo, hi),)] for lo, hi in split3(ref.shape[-1])]


def scatter_kernel(grads, *refs):
    late, (out_one, out_two) = refs[0:3], refs[3:5]
    wide, mid_one = refs[5:14], refs[14:17]
    one_mid, one_end, two_mid, two_end = (refs[17 + 3 * i : 20 + 3 * i] for i in range(4))
    mid2_one, mid2_two = refs[29:32], refs[32:35]
    ssem, rsem = refs[35:]
    place = coords()
    greet(place, EVERY)
    far, near = wide_bufs(wide)
    a = Scatter(place, column_views(grads), ssem, rsem, 0)
    b = Scatter(place, late, ssem, rsem, SCATTER_SEMS)
    a.wide_send(far)
    b.send(1, two_mid)
    a.wide_forward(far, near)
    a.wide_last(near, mid_one)
    a.send(1, one_mid)
    b.receive(1, two_mid, mid2_two)
    b.send(2, two_end)
    a.receive(1, one_mid, mid2_one)
    a.send(2, one_end)
    b.receive(2, two_end, column_views(out_two))
    a.receive(2, one_end, column_views(out_one))


def scatter_chips(grads, late, late_width, cid):
    width = grads.shape[-1]
    scratch = wide_scratch(width)
    scratch += [pltpu.VMEM(s, BF16) for s in part_shapes(width, 1)]
    for w in (width, late_width):
        for k in (1, 2):
            scratch += narrow_scratch(w, k)
    for w in (width, late_width):
        scratch += [pltpu.VMEM(s, BF16) for s in part_shapes(w, 2)]
    scratch += [pltpu.SemaphoreType.DMA((2 * SCATTER_SEMS,))] * 2
    return pl.pallas_call(
        scatter_kernel,
        out_shape=tuple(jax.ShapeDtypeStruct((16, w), F32) for w in (width, late_width)),
        in_specs=[pl.BlockSpec(memory_space=pltpu.VMEM)] * 4,
        out_specs=[pl.BlockSpec(memory_space=pltpu.VMEM)] * 2,
        scratch_shapes=scratch,
        compiler_params=pltpu.CompilerParams(
            collective_id=cid, has_side_effects=True, vmem_limit_bytes=56 * 1024 * 1024
        ),
        name="scatter",
    )(grads.reshape(2, 4, 4, 2, 16, width), *late)


def dot_nt(a, b):
    return lax.dot_general(a, b, (((1,), (1,)), ((), ())), preferred_element_type=F32)


def dot_nn(a, b):
    return lax.dot_general(a, b, (((1,), (0,)), ((), ())), preferred_element_type=F32)


def sigmoid_of(raw):
    return 1.0 / (1.0 + jnp.exp2(raw * (-LOG2E / 8.0) + 13.0))


PAIR = 2 * TILE
SPAN = 4 * TILE


def tile_rows(p):
    return pl.ds(pl.multiple_of(p * TILE, TILE), TILE)


def pair_rows(t):
    return pl.ds(pl.multiple_of(t * PAIR, PAIR), PAIR)


def query_places(z, shape, dim):
    i = lax.broadcasted_iota(jnp.int32, shape, dim)
    return z * TILE + i + jnp.where(i >= TILE, SPAN - TILE, 0)


def attend_kernel(qkv, late_in, kv_all, att, late, acc, ssem, rsem, gs, gr):
    place = coords()
    z = place["z"]
    greet(place, EVERY)

    def piece(p, j, off):
        return remote(
            qkv.at[tile_rows(p), 128:256],
            kv_all.at[p, z],
            ssem,
            rsem,
            p * 3 + j,
            step_id(place, "z", off),
        )

    def start(p, _):
        for j, off in enumerate((1, 3, 2)):
            piece(p, j, off).start()
        return 0

    lax.fori_loop(0, PERIODS, start, 0)
    gather = Gather(place, None, late, gs, gr, 0)
    gather.send(2)

    def keep(p, _):
        kv_all[p, z] = qkv[tile_rows(p), 128:256]
        return 0

    lax.fori_loop(0, PERIODS, keep, 0)

    def keys(r):
        return kv_all[r].reshape(SPAN, 128)

    def pair(t, _):
        for i in range(2):
            p = 2 * t + i
            for j, off in enumerate((3, 1, 2)):
                r = kv_all.at[p, lax.rem(z + off, 4)]
                remote(r, r, ssem, rsem, p * 3 + j, step_id(place, "z", off)).wait_recv()
        q = qkv[pair_rows(t), 0:128]
        acc[...] = jnp.zeros_like(acc)

        def earlier(r, _):
            kv = keys(r)
            acc[...] += dot_nn(sigmoid_of(dot_nt(q, kv)).astype(BF16), kv)
            return 0

        lax.fori_loop(0, 2 * t, earlier, 0)

        def edge(q, kv):
            shape = (q.shape[0], SPAN)
            seen = query_places(z, shape, 0) >= lax.broadcasted_iota(jnp.int32, shape, 1)
            w = jnp.where(seen, sigmoid_of(dot_nt(q, kv)), 0.0)
            return dot_nn(w.astype(BF16), kv)

        acc[...] += edge(q, keys(2 * t))
        acc[TILE:] += edge(q[TILE:], keys(2 * t + 1))
        att[pair_rows(t), :] = acc[...].astype(BF16)
        return 0

    lax.fori_loop(0, 3, pair, 0)
    gather.forward()
    pair(3, 0)
    gather.last()
    gather.finish()

    def end(p, _):
        for j, off in enumerate((1, 3, 2)):
            piece(p, j, off).wait_send()
        return 0

    lax.fori_loop(0, PERIODS, end, 0)


def attend(qkv, late, cid):
    n = qkv.shape[0]
    return pl.pallas_call(
        attend_kernel,
        out_shape=(
            jax.ShapeDtypeStruct((PERIODS, 4, TILE, 128), BF16),
            jax.ShapeDtypeStruct((n, 128), BF16),
            jax.ShapeDtypeStruct(late.shape, BF16),
        ),
        in_specs=[pl.BlockSpec(memory_space=pltpu.VMEM), pl.BlockSpec(memory_space=pl.ANY)],
        out_specs=[pl.BlockSpec(memory_space=pltpu.VMEM)] * 2
        + [pl.BlockSpec(memory_space=pl.ANY)],
        scratch_shapes=[
            pltpu.VMEM((PAIR, 128), F32),
            pltpu.SemaphoreType.DMA((24,)),
            pltpu.SemaphoreType.DMA((24,)),
            pltpu.SemaphoreType.DMA((GATHER_SEMS,)),
            pltpu.SemaphoreType.DMA((GATHER_SEMS,)),
        ],
        input_output_aliases={1: 2},
        compiler_params=pltpu.CompilerParams(
            collective_id=cid, has_side_effects=True, vmem_limit_bytes=48 * 1024 * 1024
        ),
        name="attend",
    )(qkv, late)


def attend_back_kernel(qkv, kv_all, da_all, grads, out, *refs):
    late = refs[0:3]
    kvt, acc, dqt, own, stage, got = refs[3:9]
    far, near = wide_bufs(refs[9:18])
    ssem, rsem, gs, gr = refs[18:]
    place = coords()
    z = place["z"]
    greet(place, EVERY)
    scatter = Scatter(place, column_views(grads), gs, gr, 0)
    scatter.wide_send(far)
    dqt[...] = jnp.zeros_like(dqt)

    def piece(r, j, off):
        return remote(
            stage.at[r, lax.rem(z + off, 4)],
            got.at[j, r],
            ssem,
            rsem,
            r * 3 + j,
            step_id(place, "z", off),
        )

    def block(rows, count, masked):
        q = qkv[rows, 0:128]
        da = da_all[rows, :]
        kv = acc_keys[0]
        sg = sigmoid_of(dot_nt(kv, q))
        if masked:
            shape = (SPAN, count)
            seen = query_places(z, shape, 1) >= lax.broadcasted_iota(jnp.int32, shape, 0)
            sg = jnp.where(seen, sg, 0.0)
        ds = (dot_nt(kv, da) * (sg * (1.0 - sg))).astype(BF16)
        acc[...] += dot_nn(ds, q) + dot_nn(sg.astype(BF16), da)
        dqt[:, rows] += dot_nn(kvt[...], ds)

    acc_keys = [None]

    def span(r, t, first):
        kv = kv_all[r].reshape(SPAN, 128)
        acc_keys[0] = kv
        kvt[...] = jnp.transpose(kv.astype(F32)).astype(BF16)
        acc[...] = jnp.zeros_like(acc)
        if first:
            block(pair_rows(t), PAIR, True)
        else:
            block(tile_rows(2 * t + 1), TILE, True)

        def later(u, _):
            acc_keys[0] = kv_all[r].reshape(SPAN, 128)
            block(pair_rows(u), PAIR, False)
            return 0

        lax.fori_loop(t + 1, PERIODS // 2, later, 0)
        stage[r] = acc[...].astype(BF16).reshape(4, TILE, 128)
        own[tile_rows(r), :] = acc[tile_rows(z), :]
        for j, off in enumerate((1, 3, 2)):
            piece(r, j, off).start()

    def keys(t, _):
        span(2 * t, t, True)
        span(2 * t + 1, t, False)
        return 0

    lax.fori_loop(0, 1, keys, 0)
    scatter.wide_forward(far, near)
    lax.fori_loop(1, PERIODS // 2, keys, 0)
    scale = jnp.where(lax.broadcasted_iota(jnp.int32, (TILE, 128), 1) < HEAD, 0.125, 1.0)

    def queries(p, _):
        out[tile_rows(p), 0:128] = (jnp.transpose(dqt[:, tile_rows(p)]) * 0.125).astype(BF16)
        return 0

    lax.fori_loop(0, PERIODS, queries, 0)
    scatter.wide_last(near, late)

    def finish(p, _):
        total = own[tile_rows(p), :]
        for j, off in enumerate((1, 3, 2)):
            piece(p, j, off).wait()
            total = total + got[j, p].astype(F32)
        out[tile_rows(p), 128:256] = (total * scale).astype(BF16)
        return 0

    lax.fori_loop(0, PERIODS, finish, 0)


def attend_back(qkv, kv_all, da, grads, cid):
    n = qkv.shape[0]
    width = grads.shape[-1]
    return pl.pallas_call(
        attend_back_kernel,
        out_shape=(jax.ShapeDtypeStruct((n, 256), BF16),)
        + tuple(jax.ShapeDtypeStruct(s, BF16) for s in part_shapes(width, 1)),
        in_specs=[pl.BlockSpec(memory_space=pltpu.VMEM)] * 4,
        out_specs=[pl.BlockSpec(memory_space=pltpu.VMEM)] * 4,
        scratch_shapes=[
            pltpu.VMEM((128, SPAN), BF16),
            pltpu.VMEM((SPAN, 128), F32),
            pltpu.VMEM((128, n), F32),
            pltpu.VMEM((n, 128), F32),
            pltpu.VMEM((PERIODS, 4, TILE, 128), BF16),
            pltpu.VMEM((3, PERIODS, TILE, 128), BF16),
        ]
        + wide_scratch(width)
        + [
            pltpu.SemaphoreType.DMA((24,)),
            pltpu.SemaphoreType.DMA((24,)),
            pltpu.SemaphoreType.DMA((SCATTER_SEMS,)),
            pltpu.SemaphoreType.DMA((SCATTER_SEMS,)),
        ],
        compiler_params=pltpu.CompilerParams(
            collective_id=cid, has_side_effects=True, vmem_limit_bytes=60 * 1024 * 1024
        ),
        name="attend_back",
    )(qkv, kv_all, da, grads.reshape(2, 4, 4, 2, 16, width))


def normalize(values):
    inverse = lax.rsqrt(jnp.mean(values * values, axis=-1, keepdims=True) + EPSILON)
    return (values * inverse, inverse)


def norm_back(grad_hat, scaled, inverse):
    return inverse * (grad_hat - scaled * jnp.mean(grad_hat * scaled, axis=-1, keepdims=True))


def outer_sum(left, right):
    return lax.dot_general(left, right, (((0,), (0,)), ((), ())), preferred_element_type=F32)


def adam_step(weight, first, second, grad, rate, decay):
    first_new = BETA_ONE * first + (1.0 - BETA_ONE) * grad
    second_new = BETA_TWO * second + (1.0 - BETA_TWO) * grad * grad
    direction = (
        first_new
        / (1.0 - BETA_ONE**STEP)
        / (jnp.sqrt(second_new / (1.0 - BETA_TWO**STEP)) + ADAM_EPS)
    )
    return (weight - rate * (direction + decay * weight), second_new)


def other_core(values):
    return lax.ppermute(values, "core", SWAP)


def both(core, values, axis):
    other = other_core(values)
    first = jnp.where(core == 0, values, other)
    last = jnp.where(core == 0, other, values)
    return jnp.concatenate([first, last], axis=axis)


def by_core(values):
    cut = values.reshape(values.shape[0], 64, 2, 22)
    main = jnp.moveaxis(cut[..., :16], 2, 0).reshape(2, values.shape[0], 1024)
    tail = jnp.moveaxis(cut[..., 16:], 2, 0).reshape(2, values.shape[0], 384)
    return jnp.concatenate([main, tail], axis=-1)


def from_cores(values):
    n = values.shape[1]
    main = jnp.moveaxis(values[..., :1024].reshape(2, n, 64, 16), 0, 2)
    tail = jnp.moveaxis(values[..., 1024:].reshape(2, n, 64, 6), 0, 2)
    return jnp.concatenate([main, tail], axis=-1).reshape(n, FF)


def pick(values, core):
    return lax.dynamic_index_in_dim(values, core, 0, keepdims=False)


def spread(offset):
    src = lax.broadcasted_iota(jnp.int32, (512, 1024), 0)
    dst = lax.broadcasted_iota(jnp.int32, (512, 1024), 1)
    return (dst == src // HEAD * 128 + src % HEAD + offset).astype(BF16)


def to_heads(values):
    n = values.shape[-1] // 8
    return values.reshape(2, 128, 8, n).transpose(0, 2, 1, 3).reshape(2048, n)


def from_heads(values):
    n = values.shape[-1]
    return values.reshape(2, 8, 128, n).transpose(0, 2, 1, 3).reshape(256, 8 * n)


def exchange(values):
    return lax.all_to_all(values, ("yl", "x", "yh"), 0, 0, tiled=True)


def dot(a, b):
    return jnp.dot(a, b, preferred_element_type=F32)


def body(
    tokens, cotangent, w_attn, w_ffn_in, w_down, gains, m_attn, m_ffn_in, m_down, m_gains,
    v_attn, v_ffn_in, v_down, v_gains,
):
    core = lax.axis_index("core")
    attn_low = w_attn.astype(BF16)
    ffn_low = w_ffn_in.astype(BF16)
    down_low = w_down.astype(BF16)
    qkv_low = attn_low[:3].reshape(3, 8, 2, 8, HEAD)
    key_value = jnp.stack([qkv_low[1], qkv_low[2]], axis=3)
    early = jnp.concatenate(
        [
            qkv_low[0].transpose(1, 0, 2, 3).reshape(2, 8, 512),
            key_value.transpose(1, 0, 2, 3, 4).reshape(2, 8, 1024),
        ],
        axis=-1,
    )
    late = jnp.concatenate([by_core(ffn_low[0]), by_core(ffn_low[1])], axis=-1)
    packed = jnp.concatenate([early, late], axis=-1)
    mine = pick(packed, core)
    theirs = other_core(pick(packed, 1 - core))
    rows16 = jnp.concatenate(
        [jnp.where(core == 0, mine, theirs), jnp.where(core == 0, theirs, mine)], axis=0
    )
    out_gain = jnp.concatenate(
        [
            attn_low[3],
            jnp.pad(gains.astype(BF16).T, ((0, 0), (0, 126))),
        ],
        axis=-1,
    )
    out_gain = both(core, out_gain, 0)
    shard_one = jnp.concatenate([rows16[:, :1536], out_gain[:, 1024:]], axis=-1)
    shard_two = jnp.concatenate(
        [rows16[:, 1536:], out_gain[:, :1024], down_low[:16], down_low[16:].reshape(16, 384)],
        axis=-1,
    )
    full_one, full_two = gather_chips(shard_one, shard_two, 1)
    full_one = full_one.reshape(1024, -1)
    w_q = full_one[:, :512]
    w_kv = full_one[:, 512:1536]
    gain_one = full_one[:, 1536].astype(F32)
    gain_two = full_one[:, 1537].astype(F32)
    inputs = both(core, tokens, 1).astype(F32).reshape(256, WIDTH)
    grad_rows = both(core, cotangent, 1).reshape(256, WIDTH)

    scaled_one, inverse_one = normalize(inputs)
    normed_one = (scaled_one * gain_one).astype(BF16)
    queries = dot(dot(normed_one, w_q).astype(BF16), spread(0)).astype(BF16)
    keys_values = dot(normed_one, w_kv).astype(BF16)
    qkv = exchange(jnp.concatenate([to_heads(queries), to_heads(keys_values)], axis=-1))
    kv_all, att, full_two = attend(qkv, full_two, 2)
    full_two = full_two.reshape(1024, -1)
    w_gate = full_two[:, :HALF]
    w_up = full_two[:, HALF : 2 * HALF]
    w_out = full_two[:, 2 * HALF : 2 * HALF + 1024]
    w_dn = jnp.concatenate(
        [
            full_two[:, 2 * HALF + 1024 : 2 * HALF + 2048],
            full_two[:, 2 * HALF + 2048 :].reshape(384, 1024),
        ],
        axis=0,
    )
    att = from_heads(exchange(att))
    att_half = lax.dot_general(
        att, spread(HEAD), (((1,), (1,)), ((), ())), preferred_element_type=F32
    ).astype(BF16)
    attn_out = both(core, att_half, 1)
    middle = inputs + dot(attn_out, w_out)
    scaled_two, inverse_two = normalize(middle)
    normed_two = (scaled_two * gain_two).astype(BF16)
    gate = dot(normed_two, w_gate)
    upward = dot(normed_two, w_up)
    hidden = (jax.nn.silu(gate) * upward).astype(BF16)
    result_part = dot(hidden, w_dn).reshape(2, 2, 64, WIDTH)
    mid_own = pick(middle.reshape(2, 2, 64, WIDTH).swapaxes(0, 1), core)
    part_own = pick(result_part.swapaxes(0, 1), core)
    part_other = other_core(pick(result_part.swapaxes(0, 1), 1 - core))
    output = (mid_own + (part_own + part_other)).astype(BF16)

    grad_dn = outer_sum(hidden, grad_rows)
    grad_hidden = dot_nt(grad_rows, w_dn)
    squash = jax.nn.sigmoid(gate)
    grad_up = (grad_hidden * jax.nn.silu(gate)).astype(BF16)
    grad_gate = (grad_hidden * upward * (squash + gate * squash * (1.0 - squash))).astype(BF16)
    grad_normed_two = dot_nt(grad_gate, w_gate) + dot_nt(grad_up, w_up)
    grad_normed_two = grad_normed_two + other_core(grad_normed_two)
    gain_grad_two = jnp.sum(grad_normed_two * scaled_two, axis=0)
    grad_middle = grad_rows.astype(F32) + norm_back(
        grad_normed_two * gain_two, scaled_two, inverse_two
    )
    branch_grad = grad_middle.astype(BF16)
    w_out_half = lax.dynamic_slice_in_dim(w_out, core * 512, 512, 0)
    grad_att = dot_nt(branch_grad, w_out_half).astype(BF16)
    grad_att = exchange(to_heads(dot(grad_att, spread(HEAD)).astype(BF16)))
    branch_half = lax.dynamic_slice_in_dim(branch_grad, core * 512, 512, 1)
    grads_two = jnp.concatenate(
        [
            outer_sum(normed_two, grad_gate).astype(BF16),
            outer_sum(normed_two, grad_up).astype(BF16),
            outer_sum(attn_out, branch_half).astype(BF16),
            grad_dn[:1024].astype(BF16),
            grad_dn[1024:].astype(BF16).reshape(1024, 384),
        ],
        axis=-1,
    )
    grad_qkv, *late_sums = attend_back(qkv, kv_all, grad_att, grads_two, 3)
    grad_qkv = exchange(grad_qkv)
    grad_q = lax.dot_general(
        from_heads(grad_qkv[:, :128]),
        spread(0),
        (((1,), (1,)), ((), ())),
        preferred_element_type=F32,
    ).astype(BF16)
    grad_kv = from_heads(grad_qkv[:, 128:])
    grad_normed_one = dot_nt(grad_q, w_q) + dot_nt(grad_kv, w_kv)
    grad_normed_one = grad_normed_one + other_core(grad_normed_one)
    gain_grad_one = jnp.sum(grad_normed_one * scaled_one, axis=0)
    grad_inputs = grad_middle + norm_back(grad_normed_one * gain_one, scaled_one, inverse_one)
    grad_inputs = pick(grad_inputs.reshape(2, 2, 64, WIDTH).swapaxes(0, 1), core)

    lanes = lax.broadcasted_iota(jnp.int32, (1024, 128), 1)
    gain_cols = jnp.where(lanes == 0, gain_grad_one[:, None], gain_grad_two[:, None])
    grads_one = jnp.concatenate(
        [
            outer_sum(normed_one, grad_q).astype(BF16),
            outer_sum(normed_one, grad_kv).astype(BF16),
            gain_cols.astype(BF16),
        ],
        axis=-1,
    )
    sum_one, sum_two = scatter_chips(grads_one, late_sums, grads_two.shape[-1], 4)

    wide = 2 * HALF + 512
    rows = jnp.concatenate([sum_two[:, :wide], sum_one[:, :1536]], axis=-1).reshape(2, 8, wide + 1536)
    mine = pick(rows, core)
    theirs = other_core(pick(rows, 1 - core))
    pair = jnp.stack([jnp.where(core == 0, mine, theirs), jnp.where(core == 0, theirs, mine)])
    ffn_part = jnp.stack([from_cores(pair[..., :HALF]), from_cores(pair[..., HALF : 2 * HALF])])
    out_part = jnp.concatenate([pair[0, :, 2 * HALF : wide], pair[1, :, 2 * HALF : wide]], axis=-1)
    q_part = pair[..., wide : wide + 512].transpose(1, 0, 2).reshape(8, 1024)
    kv_part = pair[..., wide + 512 :].reshape(2, 8, 8, 2, HEAD).transpose(3, 1, 0, 2, 4).reshape(2, 8, 1024)
    attn_part = jnp.concatenate([q_part[None], kv_part, out_part[None]], axis=0)
    down_part = jnp.concatenate(
        [sum_two[:, wide : wide + 1024], sum_two[:, wide + 1024 :].reshape(6, 1024)], axis=0
    )
    gain_part = pick(sum_one[:, 1536:1538].reshape(2, 8, 2), core).T

    new_attn, second_attn = adam_step(w_attn, m_attn, v_attn, attn_part, 0.06, 0.1)
    new_ffn, second_ffn = adam_step(w_ffn_in, m_ffn_in, v_ffn_in, ffn_part, 0.06, 0.1)
    new_dn, second_dn = adam_step(w_down, m_down, v_down, down_part, 0.04, 0.1)
    new_gn, second_gn = adam_step(gains, m_gains, v_gains, gain_part, 0.4, 0.0)
    return (
        output, grad_inputs, attn_part, ffn_part, down_part, gain_part,
        new_attn, new_ffn, new_dn, new_gn, second_attn, second_ffn, second_dn, second_gn,
    )


def solution(mesh):
    fine = Mesh(mesh.devices.reshape(2, 4, 4, 2, 2), AXES)
    rows3 = P(None, AXES, None)
    rows2 = P(AXES, None)
    cols = P(None, AXES)
    weights = (rows3, rows3, rows2, cols)
    return jax.shard_map(
        body,
        mesh=fine,
        in_specs=(rows3, rows3) + weights * 3,
        out_specs=(rows3, rows3) + weights * 3,
        check_vma=False,
    )
```

```python
import math

import jax
import jax.numpy as jnp
from jax import lax
from jax.experimental import pallas as pl
from jax.experimental.pallas import tpu as pltpu
from jax.sharding import Mesh
from jax.sharding import PartitionSpec as P

HEADS = 16
HEAD = 64
WIDTH = 1024
FF = 2816
HALF = FF // 2
STEP = 10
EPSILON = 1e-05
BETA_ONE = 0.9
BETA_TWO = 0.999
ADAM_EPS = 1e-08
F32 = jnp.float32
BF16 = jnp.bfloat16
AXES = ("yl", "x", "z", "yh", "core")
SWAP = [(0, 1), (1, 0)]
MESH_ID = pl.DeviceIdType.MESH
ORDERS = (("x", "y", "z"), ("y", "z", "x"), ("z", "x", "y"))
PERIODS = 8
TILE = 256
LOG2E = 1.4426950408889634


def coords():
    place = {a: lax.axis_index(a) for a in AXES}
    place["y"] = place["yh"] * 2 + place["yl"]
    return place


def step_id(place, axis, off):
    v = lax.rem(place[axis] + off, 4)
    if axis == "y":
        return {"yl": lax.rem(v, 2), "yh": v // 2}
    return {axis: v}


def region(place, done, axis, v):
    def pick(a):
        return slice(None) if a in done else (v if a == axis else place[a])

    y = pick("y")
    if isinstance(y, slice):
        return (y, pick("x"), pick("z"), y)
    return (lax.rem(y, 2), pick("x"), pick("z"), y // 2)


def halves(cols):
    lo, hi = cols
    mid = lo + ((hi - lo) // 128 + 1) // 2 * 128
    return (lo, mid), (mid, hi)


def split3(width):
    tiles = width // 128
    a = tiles // 5
    b = (tiles - a + 1) // 2
    return [(0, a * 128), (a * 128, (a + b) * 128), ((a + b) * 128, width)]


def greet(place, pairs):
    bar = pltpu.get_barrier_semaphore()
    for axis, off in pairs:
        pl.semaphore_signal(
            bar, inc=1, device_id=step_id(place, axis, off), device_id_type=MESH_ID
        )
    pl.semaphore_wait(bar, len(pairs))


def remote(src, dst, ssem, rsem, i, dev, at=None):
    return pltpu.make_async_remote_copy(
        src_ref=src,
        dst_ref=dst,
        send_sem=ssem.at[i],
        recv_sem=rsem.at[i if at is None else at],
        device_id=dev,
        device_id_type=MESH_ID,
    )


NEAR = [(a, o) for a in ("x", "y", "z") for o in (1, 3)]
EVERY = [(a, o) for a in ("x", "y", "z") for o in (1, 3, 2)]


class Gather:
    def __init__(self, place, shard, out, ssem, rsem, base):
        self.place, self.shard, self.out = place, shard, out
        self.ssem, self.rsem, self.base = ssem, rsem, base
        self.parts = list(zip(ORDERS, split3(out.shape[-1])))
        self.sends = []

    def at(self, idx, cols):
        return self.out.at[idx + (slice(None), slice(cols[0], cols[1]))]

    def copy(self, src, dst, i, axis, off):
        return remote(
            src, dst, self.ssem, self.rsem, self.base + i, step_id(self.place, axis, off)
        )

    def where(self, k, order, off):
        return region(self.place, order[:k], order[k], lax.rem(self.place[order[k]] + off, 4))

    def send(self, k):
        for p, (order, cols) in enumerate(self.parts):
            dst = self.at(self.where(k, order, 0), cols)
            src = self.shard.at[:, cols[0] : cols[1]] if k == 0 else dst
            for j, off in enumerate((1, 3, 2) if k < 2 else (1, 3)):
                d = self.copy(src, dst, k * 9 + p * 3 + j, order[k], off)
                d.start()
                self.sends.append(d)

    def receive(self, k):
        for p, (order, cols) in enumerate(self.parts):
            for j, off in enumerate((3, 1, 2)):
                r = self.at(self.where(k, order, off), cols)
                self.copy(r, r, k * 9 + p * 3 + j, order[k], off).wait_recv()

    def forward(self):
        for p, (order, cols) in enumerate(self.parts):
            for j, (off, half) in enumerate(zip((3, 1), halves(cols))):
                idx = self.where(2, order, off)
                r = self.at(idx, cols)
                self.copy(r, r, 18 + p * 3 + j, order[2], off).wait_recv()
                r = self.at(idx, half)
                d = self.copy(r, r, 27 + p * 2 + j, order[2], 4 - off)
                d.start()
                self.sends.append(d)

    def last(self):
        for p, (order, cols) in enumerate(self.parts):
            far = self.where(2, order, 2)
            for j, half in enumerate(halves(cols)):
                r = self.at(far, half)
                self.copy(r, r, 27 + p * 2 + j, order[2], 1).wait_recv()

    def finish(self):
        for d in self.sends:
            d.wait_send()
        self.sends = []


GATHER_SEMS = 33


def part_dims(left):
    return tuple(n for n, a in zip((2, 4, 4, 2), ("y", "x", "z", "y")) if a in left)


def part_shapes(width, k):
    return [
        part_dims(order[::-1][k:]) + (16, hi - lo)
        for order, (lo, hi) in zip(ORDERS, split3(width))
    ]


def sum_blocks(target, terms):
    dims = target.shape[:-2]

    def one(i, _):
        idx = []
        for n in reversed(dims):
            idx.append(lax.rem(i, n))
            i = i // n
        idx = tuple(reversed(idx))
        total = terms[0][idx].astype(F32)
        for t in terms[1:]:
            total = total + t[idx].astype(F32)
        target[idx] = total.astype(target.dtype)
        return 0

    if dims:
        lax.fori_loop(0, math.prod(dims), one, 0)
    else:
        one(0, 0)


class Scatter:
    def __init__(self, place, views, ssem, rsem, base):
        self.place, self.views = place, views
        self.ssem, self.rsem, self.base = ssem, rsem, base
        self.sends = []

    def copy(self, src, dst, i, axis, off):
        return remote(
            src, dst, self.ssem, self.rsem, self.base + i, step_id(self.place, axis, off)
        )

    def chunk(self, p, k, off, cols=None):
        back = ORDERS[p][::-1]
        idx = region(
            self.place, back[k + 1 :], back[k], lax.rem(self.place[back[k]] + off, 4)
        )
        if k > 0:
            gone = back[:k]
            idx = tuple(
                i for i, a in zip(idx, ("y", "x", "z", "y")) if a not in gone
            )
        view = self.views[p]
        lo, hi = cols or (0, view.shape[-1])
        return view.at[idx + (slice(None), slice(lo, hi))]

    def cut(self, p):
        return halves((0, self.views[p].shape[-1]))

    def wide_send(self, far):
        for p in range(3):
            axis = ORDERS[p][2]
            for j, (off, half) in enumerate(zip((1, 3), self.cut(p))):
                d = self.copy(self.chunk(p, 0, 2, half), far[p][j], p * 4 + j, axis, off)
                d.start()
                self.sends.append(d)

    def wide_forward(self, far, near):
        for p in range(3):
            axis = ORDERS[p][2]
            cut = self.cut(p)
            for j, off in enumerate((1, 3)):
                got = far[p][j]
                self.copy(got, got, p * 4 + j, axis, 4 - off).wait_recv()
                sum_blocks(got, [got, self.chunk(p, 0, off, cut[j])])
                for i, src in ((j, got), (1 - j, self.chunk(p, 0, off, cut[1 - j]))):
                    lo, hi = cut[i]
                    n = len(near[p].shape) - 2
                    dst = near[p].at[(j,) + (slice(None),) * n + (slice(lo, hi),)]
                    d = self.copy(src, dst, 12 + p * 4 + j * 2 + (i != j), axis, off)
                    d.start()
                    self.sends.append(d)

    def wide_last(self, near, out):
        for p in range(3):
            axis = ORDERS[p][2]
            cut = self.cut(p)
            n = len(near[p].shape) - 2
            for j, off in enumerate((1, 3)):
                for i in (j, 1 - j):
                    lo, hi = cut[i]
                    dst = near[p].at[(j,) + (slice(None),) * n + (slice(lo, hi),)]
                    self.copy(dst, dst, 12 + p * 4 + j * 2 + (i != j), axis, 4 - off).wait_recv()
            sum_blocks(out[p], [self.chunk(p, 0, 0), near[p].at[0], near[p].at[1]])
        self.finish()
        self.views = out

    def send(self, k, bufs):
        for p in range(3):
            axis = ORDERS[p][2 - k]
            for j, off in enumerate((1, 3, 2)):
                i = 24 + (k - 1) * 9 + p * 3 + j
                d = self.copy(self.chunk(p, k, off), bufs[p].at[j], i, axis, off)
                d.start()
                self.sends.append(d)

    def receive(self, k, bufs, out):
        for p in range(3):
            axis = ORDERS[p][2 - k]
            for j, off in enumerate((1, 3, 2)):
                r = bufs[p].at[j]
                self.copy(r, r, 24 + (k - 1) * 9 + p * 3 + j, axis, 4 - off).wait_recv()
            sum_blocks(out[p], [self.chunk(p, k, 0)] + [bufs[p].at[j] for j in range(3)])
        self.finish()
        self.views = out

    def finish(self):
        for d in self.sends:
            d.wait_send()
        self.sends = []


SCATTER_SEMS = 42


def wide_scratch(width):
    far, near = [], []
    for shape in part_shapes(width, 1):
        for lo, hi in halves((0, shape[-1])):
            far.append(pltpu.VMEM(shape[:-1] + (hi - lo,), BF16))
        near.append(pltpu.VMEM((2,) + shape, BF16))
    return far + near


def narrow_scratch(width, k):
    return [pltpu.VMEM((3,) + shape, BF16) for shape in part_shapes(width, k + 1)]


def wide_bufs(refs):
    return [refs[2 * p : 2 * p + 2] for p in range(3)], refs[6:9]


def column_views(ref):
    whole = (slice(None),) * (len(ref.shape) - 1)
    return [ref.at[whole + (slice(lo, hi),)] for lo, hi in split3(ref.shape[-1])]


def dot_nt(a, b):
    return lax.dot_general(a, b, (((1,), (1,)), ((), ())), preferred_element_type=F32)


def dot_nn(a, b):
    return lax.dot_general(a, b, (((1,), (0,)), ((), ())), preferred_element_type=F32)


def sigmoid_of(raw):
    return 1.0 / (1.0 + jnp.exp2(raw * (-LOG2E / 8.0) + 13.0))


PAIR = 2 * TILE
SPAN = 4 * TILE


def tile_rows(p):
    return pl.ds(pl.multiple_of(p * TILE, TILE), TILE)


def pair_rows(t):
    return pl.ds(pl.multiple_of(t * PAIR, PAIR), PAIR)


def query_places(z, shape, dim):
    i = lax.broadcasted_iota(jnp.int32, shape, dim)
    return z * TILE + i + jnp.where(i >= TILE, SPAN - TILE, 0)


def unit_of(place):
    return (place["yl"] * 4 + place["x"]) * 2 + place["yh"]


def unit_id(g):
    return {"yl": g // 8, "x": lax.rem(g // 2, 4), "yh": lax.rem(g, 2)}


def greet_all(place):
    me = unit_of(place)
    devices = [unit_id(lax.rem(me + i, 16)) for i in range(1, 16)]
    for off in (1, 2, 3):
        z = step_id(place, "z", off)
        devices += [z, {"yl": 1 - place["yl"], **z}]
    devices.append({"core": 1 - place["core"]})
    bar = pltpu.get_barrier_semaphore()
    for dev in devices:
        pl.semaphore_signal(bar, inc=1, device_id=dev, device_id_type=MESH_ID)
    pl.semaphore_wait(bar, len(devices))


SIDES = [(a, b) for a in range(2) for b in range(4) if (a, b) != (0, 0)]


def side_id(place, side):
    return {
        "yl": lax.rem(place["yl"] + side[0], 2),
        "z": lax.rem(place["z"] + side[1], 4),
    }


def from_side(place, side):
    return lax.rem(place["yl"] + side[0], 2), lax.rem(place["z"] + 4 - side[1], 4)


def spread(offset):
    src = lax.broadcasted_iota(jnp.int32, (128, 256), 0)
    dst = lax.broadcasted_iota(jnp.int32, (128, 256), 1)
    return (dst == src + offset + jnp.where(src >= HEAD, HEAD, 0)).astype(BF16)


def rows128(g):
    return pl.ds(pl.multiple_of(g * 128, 128), 128)


def lanes(start, count):
    return pl.ds(pl.multiple_of(start, 128), count)


def columns(ref, start, count):
    return ref[:, :, :, :, :, lanes(start, count)].reshape(1024, count)


def front_kernel(
    tokens, cotangent, slices, two,
    xs, ys, normed, qkv, kv_all, att, gains, late,
    rows, mid, wsib, wpack, wfull, send_att, got_att, acc,
    lsem, pair_s, pair_r, gs, gr, xs_, xr, ws, wr, ks, kr, as_, ar,
):
    place = coords()
    z, core, me = place["z"], place["core"], unit_of(place)
    yl, x, yh = place["yl"], place["x"], place["yh"]
    head = x * 2 + yh
    other = {"core": 1 - core}
    own = late.at[yl, x, z, yh]
    load = pltpu.make_async_copy(two, own, lsem.at[0])
    load.start()
    second = Gather(place, two, late, gs, gr, 0)
    cut = WIDTH // 2
    greet_all(place)
    started = []

    def go(src, dst, ssem, rsem, i, dev):
        d = remote(src, dst, ssem, rsem, i, dev)
        d.start()
        started.append(d)

    def to_y(off):
        y = lax.rem(place["y"] + off, 4)
        return lax.rem(y, 2), y // 2

    go(slices.at[1 - core], wsib, ws, wr, 0, other)
    for j, off in enumerate((1, 3, 2)):
        go(
            tokens.at[to_y(off)[0], :, 0:cut],
            rows.at[yl, x, yh, core, :, 0:cut],
            xs_, xr, j, step_id(place, "y", off),
        )
        go(
            tokens.at[:, :, cut:WIDTH], mid.at[:, x], xs_, xr, 3 + j, step_id(place, "x", off)
        )
    mine = pl.ds(pl.multiple_of(core * 64, 64), 64)
    for i, (src, dst) in enumerate(((tokens, xs), (cotangent, ys))):
        go(src, dst.at[:, mine], pair_s, pair_r, i, other)
        dst[:, mine] = src[...]
    rows[yl, x, yh, core] = tokens[yl]
    mid[:, x] = tokens[:, :, cut:WIDTH]
    second.send(0)

    remote(wsib, wsib, ws, wr, 0, other).wait_recv()
    for h in range(8):
        a, b = slices[core, h], wsib[h]
        wpack[h] = jnp.concatenate(
            [jnp.where(core == 0, a, b), jnp.where(core == 0, b, a)], axis=0
        ).astype(BF16)
    for i in range(1, 8):
        h = lax.rem(head + i, 8)
        go(
            wpack.at[h], wfull.at[yl, x, z, yh], ws, wr, i,
            {"x": h // 2, "yh": lax.rem(h, 2)},
        )
    wfull[yl, x, z, yh] = wpack[head]

    for j, off in enumerate((3, 1, 2)):
        a, b = to_y(off)
        r = rows.at[a, x, b, core, :, 0:cut]
        remote(r, r, xs_, xr, j, step_id(place, "y", off)).wait_recv()
    r = rows.at[:, x, :, core, :, 0:cut]
    for j, off in enumerate((1, 3, 2)):
        go(r, r, xs_, xr, 6 + j, step_id(place, "x", off))
    go(r, r, xs_, xr, 12, other)
    for j, off in enumerate((3, 1, 2)):
        r = mid.at[:, lax.rem(x + off, 4)]
        remote(r, r, xs_, xr, 3 + j, step_id(place, "x", off)).wait_recv()
    r = rows.at[yl, :, yh, core, :, cut:WIDTH]
    for j, off in enumerate((1, 3, 2)):
        go(mid.at[to_y(off)[0]], r, xs_, xr, 9 + j, step_id(place, "y", off))
    rows[yl, :, yh, core, :, cut:WIDTH] = mid[yl]
    go(r, r, xs_, xr, 16, other)

    for i in range(1, 8):
        h = lax.rem(head + 8 - i, 8)
        r = wfull.at[yl, h // 2, z, lax.rem(h, 2)]
        remote(r, r, ws, wr, i, other).wait_recv()
    r = wfull.at[yl, :, z]
    for i, side in enumerate(SIDES):
        go(r, r, ws, wr, 8 + i, side_id(place, side))
    load.wait()
    second.receive(0)
    second.send(1)

    for j, off in enumerate((3, 1, 2)):
        r = rows.at[:, lax.rem(x + off, 4), :, core, :, 0:cut]
        remote(r, r, xs_, xr, 6 + j, step_id(place, "x", off)).wait_recv()
        go(r, r, xs_, xr, 13 + j, other)
    for j, off in enumerate((3, 1, 2)):
        a, b = to_y(off)
        r = rows.at[a, :, b, core, :, cut:WIDTH]
        remote(r, r, xs_, xr, 9 + j, step_id(place, "y", off)).wait_recv()
        go(r, r, xs_, xr, 17 + j, other)
    for i, side in enumerate(SIDES):
        a, b = from_side(place, side)
        r = wfull.at[a, :, b]
        remote(r, r, ws, wr, 8 + i, other).wait_recv()
    second.receive(1)
    second.send(2)
    for j, off in enumerate((0, 3, 1, 2)):
        r = rows.at[:, lax.rem(x + off, 4), :, 1 - core, :, 0:cut]
        remote(r, r, xs_, xr, 12 + j, other).wait_recv()
    for j, off in enumerate((0, 3, 1, 2)):
        a, b = to_y(off)
        r = rows.at[a, :, b, 1 - core, :, cut:WIDTH]
        remote(r, r, xs_, xr, 16 + j, other).wait_recv()

    lane = lax.broadcasted_iota(jnp.int32, (8, 128), 1)
    pick_lane = lane == lax.broadcasted_iota(jnp.int32, (8, 128), 0)
    gains[...] = dot_nt(pick_lane.astype(BF16), columns(wfull, 256, 128))

    def piece(p, j, off):
        return remote(
            qkv.at[tile_rows(p), 128:256],
            kv_all.at[p, z],
            ks,
            kr,
            p * 3 + j,
            step_id(place, "z", off),
        )

    def project(p, _):
        block = rows[p // 4, lax.rem(p, 4)].reshape(TILE, WIDTH).astype(F32)
        h = (normalize(block)[0] * gains[0:1]).astype(BF16)
        normed[tile_rows(p), :] = h
        qkv[tile_rows(p), :] = dot_nn(h, columns(wfull, 0, 256)).astype(BF16)
        for j, off in enumerate((1, 3, 2)):
            piece(p, j, off).start()
        kv_all[p, z] = qkv[tile_rows(p), 128:256]
        return 0

    lax.fori_loop(0, PERIODS, project, 0)

    def keys(r):
        return kv_all[r].reshape(SPAN, 128)

    def pair(t, _):
        for i in range(2):
            p = 2 * t + i
            for j, off in enumerate((3, 1, 2)):
                r = kv_all.at[p, lax.rem(z + off, 4)]
                remote(r, r, ks, kr, p * 3 + j, step_id(place, "z", off)).wait_recv()
        q = qkv[pair_rows(t), 0:128]
        acc[...] = jnp.zeros_like(acc)

        def earlier(r, _):
            kv = keys(r)
            acc[...] += dot_nn(sigmoid_of(dot_nt(q, kv)).astype(BF16), kv)
            return 0

        lax.fori_loop(0, 2 * t, earlier, 0)

        def edge(q, kv):
            shape = (q.shape[0], SPAN)
            seen = query_places(z, shape, 0) >= lax.broadcasted_iota(jnp.int32, shape, 1)
            w = jnp.where(seen, sigmoid_of(dot_nt(q, kv)), 0.0)
            return dot_nn(w.astype(BF16), kv)

        acc[...] += edge(q, keys(2 * t))
        acc[TILE:] += edge(q[TILE:], keys(2 * t + 1))
        for i in range(4):
            g = 4 * t + i
            send_att[g] = acc[i * 128 : i * 128 + 128].astype(BF16)

            @pl.when(g != me)
            def _():
                remote(send_att.at[g], got_att.at[me], as_, ar, g, unit_id(g), me).start()

            @pl.when(g == me)
            def _():
                got_att[me] = send_att[g]

        return 0

    lax.fori_loop(0, 3, pair, 0)
    second.forward()
    pair(3, 0)

    def end(g, _):
        @pl.when(g != me)
        def _():
            r = got_att.at[g]
            remote(r, r, as_, ar, g, unit_id(g), g).wait_recv()
            remote(send_att.at[g], r, as_, ar, g, unit_id(g), g).wait_send()

        return 0

    lax.fori_loop(0, 16, end, 0)
    for j in range(4):
        for seq in range(2):
            g = seq * 8 + j * 2
            two_heads = jnp.concatenate([got_att[g], got_att[g + 1]], axis=1)
            att[seq * 128 : seq * 128 + 128, lanes(core * 512 + j * 128, 128)] = dot_nt(
                two_heads, spread(HEAD)
            ).astype(BF16)
    r = att.at[:, lanes(core * 512, 512)]
    go(r, r, pair_s, pair_r, 2, other)
    for i, ref in enumerate((xs, ys)):
        r = ref.at[:, pl.ds(pl.multiple_of((1 - core) * 64, 64), 64)]
        remote(r, r, pair_s, pair_r, i, other).wait_recv()
    second.last()
    second.finish()

    def sent(p, _):
        for j, off in enumerate((1, 3, 2)):
            piece(p, j, off).wait_send()
        return 0

    lax.fori_loop(0, PERIODS, sent, 0)
    for d in started:
        d.wait_send()
    r = att.at[:, lanes((1 - core) * 512, 512)]
    remote(r, r, pair_s, pair_r, 2, other).wait_recv()


def dma_sems(*counts):
    return [pltpu.SemaphoreType.DMA((n,)) for n in counts]


def front(tokens, cotangent, slices, two, cid):
    lead = (2, 4, 4, 2)
    n = PERIODS * TILE
    vmem = pl.BlockSpec(memory_space=pltpu.VMEM)
    hbm = pl.BlockSpec(memory_space=pl.ANY)
    return pl.pallas_call(
        front_kernel,
        out_shape=(
            jax.ShapeDtypeStruct((2, 128, WIDTH), BF16),
            jax.ShapeDtypeStruct((2, 128, WIDTH), BF16),
            jax.ShapeDtypeStruct((n, WIDTH), BF16),
            jax.ShapeDtypeStruct((n, 256), BF16),
            jax.ShapeDtypeStruct((PERIODS, 4, TILE, 128), BF16),
            jax.ShapeDtypeStruct((256, WIDTH), BF16),
            jax.ShapeDtypeStruct((8, WIDTH), F32),
            jax.ShapeDtypeStruct(lead + two.shape, BF16),
        ),
        in_specs=[vmem] * 3 + [hbm],
        out_specs=[vmem] * 7 + [hbm],
        scratch_shapes=[
            pltpu.VMEM((2, 4, 2, 2, 64, WIDTH), BF16),
            pltpu.VMEM((2, 4, 64, WIDTH // 2), BF16),
            pltpu.VMEM((8, 8, 384), F32),
            pltpu.VMEM((8, 16, 384), BF16),
            pltpu.VMEM(lead + (16, 384), BF16),
            pltpu.VMEM((16, 128, 128), BF16),
            pltpu.VMEM((16, 128, 128), BF16),
            pltpu.VMEM((PAIR, 128), F32),
        ]
        + dma_sems(1, 3, 3, GATHER_SEMS, GATHER_SEMS, 20, 20, 15, 15, 24, 24, 16, 16),
        compiler_params=pltpu.CompilerParams(
            collective_id=cid, has_side_effects=True, vmem_limit_bytes=56 * 1024 * 1024
        ),
        name="front",
    )(tokens, cotangent, slices, two)


def back_kernel(
    qkv, kv_all, normed, da_half, grads, wqkv, dw_out, dh_out, sum_out, *refs
):
    (kvt, acc, dqt, dkvt, own, stage, got, da_all, send_da, send_q, send_kv, ret_q, ret_kv) = refs[:13]
    dw, dw_got, dw_sum, dw_head, part, part_got = refs[13:19]
    far, near = wide_bufs(refs[19:28])
    mid, buf_one, mid_one, buf_two = (refs[28 + 3 * i : 31 + 3 * i] for i in range(4))
    ssem, rsem, gs, gr, das, dar, qs, qr, kvs, kvr, ws, wr = refs[40:]
    place = coords()
    z, core, me = place["z"], place["core"], unit_of(place)
    yl, x, yh = place["yl"], place["x"], place["yh"]
    head = x * 2 + yh
    other = {"core": 1 - core}
    greet_all(place)

    def swap_out(src, dst, sems, g):
        @pl.when(g != me)
        def _():
            remote(src, dst.at[me], *sems, g, unit_id(g), me).start()

        @pl.when(g == me)
        def _():
            dst[me] = src[...]

    def swap_in(dst, sems, g):
        @pl.when(g != me)
        def _():
            r = dst.at[g]
            remote(r, r, *sems, g, unit_id(g), g).wait_recv()

    def swap_end(src, sems):
        def one(g, _):
            @pl.when(g != me)
            def _():
                remote(src.at[g], src.at[g], *sems, g, unit_id(g), g).wait_send()

            return 0

        lax.fori_loop(0, 16, one, 0)

    def give(j, _):
        two_heads = dot_nn(da_half[:, lanes(j * 128, 128)], spread(HEAD)).astype(BF16)
        for seq in range(2):
            for i in range(2):
                g = seq * 8 + j * 2 + i
                send_da[g] = two_heads[seq * 128 : seq * 128 + 128, i * 128 : i * 128 + 128]
                swap_out(send_da.at[g], da_all, (das, dar), g)
        return 0

    lax.fori_loop(0, 4, give, 0)
    scatter = Scatter(place, column_views(grads), gs, gr, 0)
    scatter.wide_send(far)
    dqt[...] = jnp.zeros_like(dqt)

    def piece(r, j, off):
        return remote(
            stage.at[r, lax.rem(z + off, 4)],
            got.at[j, r],
            ssem,
            rsem,
            r * 3 + j,
            step_id(place, "z", off),
        )

    def block(kv, first, count, masked):
        here = pl.ds(pl.multiple_of(first, TILE), count)
        q = qkv[here, 0:128]
        da = da_all[pl.ds(first // 128, count // 128)].reshape(count, 128)
        sg = sigmoid_of(dot_nt(kv, q))
        if masked:
            shape = (SPAN, count)
            seen = query_places(z, shape, 1) >= lax.broadcasted_iota(jnp.int32, shape, 0)
            sg = jnp.where(seen, sg, 0.0)
        ds = (dot_nt(kv, da) * (sg * (1.0 - sg))).astype(BF16)
        acc[...] += dot_nn(ds, q) + dot_nn(sg.astype(BF16), da)
        dqt[:, here] += dot_nn(kvt[...], ds)

    def span(r, t, first, begin):
        kv = kv_all[r].reshape(SPAN, 128)
        kvt[...] = jnp.transpose(kv.astype(F32)).astype(BF16)
        acc[...] = jnp.zeros_like(acc)

        def await_pair(u):
            if begin:
                for i in range(4):
                    swap_in(da_all, (das, dar), 4 * u + i)

        await_pair(t)
        if first:
            block(kv, t * PAIR, PAIR, True)
        else:
            block(kv, t * PAIR + TILE, TILE, True)

        def later(u, _):
            await_pair(u)
            block(kv_all[r].reshape(SPAN, 128), u * PAIR, PAIR, False)
            return 0

        lax.fori_loop(t + 1, PERIODS // 2, later, 0)
        stage[r] = acc[...].astype(BF16).reshape(4, TILE, 128)
        own[tile_rows(r), :] = acc[tile_rows(z), :]
        for j, off in enumerate((1, 3, 2)):
            piece(r, j, off).start()

    scale = jnp.where(lax.broadcasted_iota(jnp.int32, (TILE, 128), 1) < HEAD, 0.125, 1.0)

    def settle(p):
        total = own[tile_rows(p), :]
        for j, off in enumerate((1, 3, 2)):
            piece(p, j, off).wait()
            total = total + got[j, p].astype(F32)
        total = total * scale
        dkvt[:, tile_rows(p)] = jnp.transpose(total).astype(BF16)
        for i in range(2):
            g = 2 * p + i
            send_kv[g] = total[i * 128 : i * 128 + 128].astype(BF16)
            swap_out(send_kv.at[g], ret_kv, (kvs, kvr), g)

    def queries(t):
        done = jnp.transpose(dqt[:, pair_rows(t)]) * 0.125
        for i in range(4):
            g = 4 * t + i
            send_q[g] = done[i * 128 : i * 128 + 128].astype(BF16)
            swap_out(send_q.at[g], ret_q, (qs, qr), g)

    span(0, 0, True, True)
    span(1, 0, False, False)
    queries(0)
    scatter.wide_forward(far, near)

    def keys(t, _):
        span(2 * t, t, True, False)
        span(2 * t + 1, t, False, False)
        queries(t)
        settle(2 * t - 2)
        settle(2 * t - 1)
        return 0

    lax.fori_loop(1, PERIODS // 2, keys, 0)
    scatter.wide_last(near, mid)
    scatter.send(1, buf_one)
    settle(PERIODS - 2)
    settle(PERIODS - 1)

    def outer(n, _):
        h = normed[:, lanes(n * 256, 256)]
        for i, left in enumerate(((dqt[...] * 0.125).astype(BF16), dkvt[...])):
            rows = jnp.transpose(dot_nn(left, h)).astype(BF16).reshape(2, 4, 2, 16, 128)
            dw[n // 2, pl.ds(lax.rem(n, 2) * 2, 2), :, :, :, i * 128 : i * 128 + 128] = rows
        return 0

    lax.fori_loop(0, 4, outer, 0)
    started = []

    def go(src, dst, ssem, rsem, i, dev):
        d = remote(src, dst, ssem, rsem, i, dev)
        d.start()
        started.append(d)

    for i, side in enumerate(SIDES):
        dev = side_id(place, side)
        go(dw.at[dev["yl"], :, dev["z"]], dw_got.at[i], ws, wr, i, dev)

    def take(g, _):
        swap_in(ret_q, (qs, qr), g)
        swap_in(ret_kv, (kvs, kvr), g)
        return 0

    lax.fori_loop(0, 16, take, 0)
    dq, dkv = [], []
    for seq in range(2):
        base = seq * 8
        dq.append(
            jnp.concatenate(
                [
                    dot_nt(
                        jnp.concatenate([ret_q[base + 2 * j], ret_q[base + 2 * j + 1]], axis=1),
                        spread(0),
                    ).astype(BF16)
                    for j in range(4)
                ],
                axis=1,
            )
        )
        dkv.append(jnp.concatenate([ret_kv[base + j] for j in range(8)], axis=1))
    dq = jnp.concatenate(dq, axis=0)
    dkv = jnp.concatenate(dkv, axis=0)
    for n in range(4):
        w = wqkv[n * 256 : n * 256 + 256, :]
        total = dot_nt(dq, w[:, :512]) + dot_nt(dkv, w[:, 512:])
        part[:, :, :, n * 256 : n * 256 + 256] = total.reshape(2, 2, 64, 256)
    go(part.at[:, 1 - core], part_got, ws, wr, 7, other)

    total = dw[yl, :, z].astype(F32)
    for i, side in enumerate(SIDES):
        r = dw_got.at[i]
        remote(r, r, ws, wr, i, other).wait_recv()
        total = total + dw_got[i].astype(F32)
    dw_sum[...] = total.reshape(8, 16, 256)
    for i in range(1, 8):
        h = lax.rem(head + i, 8)
        go(
            dw_sum.at[h], dw_head.at[head], ws, wr, 8 + i,
            {"x": h // 2, "yh": lax.rem(h, 2)},
        )
    dw_head[head] = dw_sum[head]
    scatter.receive(1, buf_one, mid_one)
    scatter.send(2, buf_two)
    for i in range(1, 8):
        h = lax.rem(head + 8 - i, 8)
        r = dw_head.at[h]
        remote(r, r, ws, wr, 8 + i, other).wait_recv()
    theirs = pl.ds(pl.multiple_of((1 - core) * 8, 8), 8)
    go(dw_head.at[:, theirs], dw_out.at[core], ws, wr, 8, other)
    dw_out[core] = dw_head[:, pl.ds(pl.multiple_of(core * 8, 8), 8)]
    remote(part_got, part_got, ws, wr, 7, other).wait_recv()
    dh_out[...] = part[:, core] + part_got[...]
    scatter.receive(2, buf_two, column_views(sum_out))
    r = dw_out.at[1 - core]
    remote(r, r, ws, wr, 8, other).wait_recv()
    for d in started:
        d.wait_send()
    for src, sems in ((send_da, (das, dar)), (send_q, (qs, qr)), (send_kv, (kvs, kvr))):
        swap_end(src, sems)


def back(qkv, kv_all, normed, da, grads, wqkv, cid):
    n = qkv.shape[0]
    width = grads.shape[-1]
    lead = (2, 4, 4, 2)
    vmem = pl.BlockSpec(memory_space=pltpu.VMEM)
    blocks = pltpu.VMEM((16, 128, 128), BF16)
    return pl.pallas_call(
        back_kernel,
        out_shape=(
            jax.ShapeDtypeStruct((2, 8, 8, 256), F32),
            jax.ShapeDtypeStruct((2, 64, WIDTH), F32),
            jax.ShapeDtypeStruct((16, width), F32),
        ),
        in_specs=[vmem] * 6,
        out_specs=[vmem] * 3,
        scratch_shapes=[
            pltpu.VMEM((128, SPAN), BF16),
            pltpu.VMEM((SPAN, 128), F32),
            pltpu.VMEM((128, n), F32),
            pltpu.VMEM((128, n), BF16),
            pltpu.VMEM((n, 128), F32),
            pltpu.VMEM((PERIODS, 4, TILE, 128), BF16),
            pltpu.VMEM((3, PERIODS, TILE, 128), BF16),
        ]
        + [blocks] * 6
        + [
            pltpu.VMEM(lead + (16, 256), BF16),
            pltpu.VMEM((7, 4, 2, 16, 256), BF16),
            pltpu.VMEM((8, 16, 256), F32),
            pltpu.VMEM((8, 16, 256), F32),
            pltpu.VMEM((2, 2, 64, WIDTH), F32),
            pltpu.VMEM((2, 64, WIDTH), F32),
        ]
        + wide_scratch(width)
        + [pltpu.VMEM(s, BF16) for s in part_shapes(width, 1)]
        + narrow_scratch(width, 1)
        + [pltpu.VMEM(s, BF16) for s in part_shapes(width, 2)]
        + narrow_scratch(width, 2)
        + dma_sems(24, 24, SCATTER_SEMS, SCATTER_SEMS, 16, 16, 16, 16, 16, 16, 16, 16),
        compiler_params=pltpu.CompilerParams(
            collective_id=cid, has_side_effects=True, vmem_limit_bytes=61 * 1024 * 1024
        ),
        name="back",
    )(qkv, kv_all, normed, da, grads.reshape(lead + (16, width)), wqkv)


def normalize(values):
    inverse = lax.rsqrt(jnp.mean(values * values, axis=-1, keepdims=True) + EPSILON)
    return (values * inverse, inverse)


def norm_back(grad_hat, scaled, inverse):
    return inverse * (grad_hat - scaled * jnp.mean(grad_hat * scaled, axis=-1, keepdims=True))


def outer_sum(left, right):
    return lax.dot_general(left, right, (((0,), (0,)), ((), ())), preferred_element_type=F32)


def adam_step(weight, first, second, grad, rate, decay):
    first_new = BETA_ONE * first + (1.0 - BETA_ONE) * grad
    second_new = BETA_TWO * second + (1.0 - BETA_TWO) * grad * grad
    direction = (
        first_new
        / (1.0 - BETA_ONE**STEP)
        / (jnp.sqrt(second_new / (1.0 - BETA_TWO**STEP)) + ADAM_EPS)
    )
    return (weight - rate * (direction + decay * weight), second_new)


def other_core(values):
    return lax.ppermute(values, "core", SWAP)


def both(core, values, axis):
    other = other_core(values)
    first = jnp.where(core == 0, values, other)
    last = jnp.where(core == 0, other, values)
    return jnp.concatenate([first, last], axis=axis)


def by_core(values):
    cut = values.reshape(values.shape[0], 64, 2, 22)
    main = jnp.moveaxis(cut[..., :16], 2, 0).reshape(2, values.shape[0], 1024)
    tail = jnp.moveaxis(cut[..., 16:], 2, 0).reshape(2, values.shape[0], 384)
    return jnp.concatenate([main, tail], axis=-1)


def from_cores(values):
    n = values.shape[1]
    main = jnp.moveaxis(values[..., :1024].reshape(2, n, 64, 16), 0, 2)
    tail = jnp.moveaxis(values[..., 1024:].reshape(2, n, 64, 6), 0, 2)
    return jnp.concatenate([main, tail], axis=-1).reshape(n, FF)


def pick(values, core):
    return lax.dynamic_index_in_dim(values, core, 0, keepdims=False)


def dot(a, b):
    return jnp.dot(a, b, preferred_element_type=F32)


def body(
    tokens, cotangent, w_attn, w_ffn_in, w_down, gains, m_attn, m_ffn_in, m_down, m_gains,
    v_attn, v_ffn_in, v_down, v_gains,
):
    core = lax.axis_index("core")
    attn_low = w_attn.astype(BF16)
    ffn_low = w_ffn_in.astype(BF16)
    down_low = w_down.astype(BF16)
    gains_low = gains.astype(BF16)
    by_head = attn_low[:3].astype(F32).reshape(3, 8, 2, 8, HEAD).transpose(2, 3, 1, 0, 4)
    none = jnp.zeros((2, 8, 8, HEAD), F32)
    gain_cols = jnp.broadcast_to(gains_low.astype(F32).T, (2, 8, 8, 2))
    slices = jnp.concatenate(
        [
            by_head[..., 0, :], none, by_head[..., 1, :], by_head[..., 2, :],
            jnp.pad(gain_cols, ((0, 0), (0, 0), (0, 0), (0, 126))),
        ],
        axis=-1,
    )
    qkv_low = attn_low[:3].reshape(3, 8, 2, 8, HEAD)
    key_value = jnp.stack([qkv_low[1], qkv_low[2]], axis=3)
    packed = jnp.concatenate(
        [
            by_core(ffn_low[0]),
            by_core(ffn_low[1]),
            qkv_low[0].transpose(1, 0, 2, 3).reshape(2, 8, 512),
            key_value.transpose(1, 0, 2, 3, 4).reshape(2, 8, 1024),
        ],
        axis=-1,
    )
    mine = pick(packed, core)
    theirs = other_core(pick(packed, 1 - core))
    rows16 = jnp.concatenate(
        [jnp.where(core == 0, mine, theirs), jnp.where(core == 0, theirs, mine)], axis=0
    )
    shard = jnp.concatenate(
        [rows16, both(core, attn_low[3], 0), down_low[:16], down_low[16:].reshape(16, 384)],
        axis=-1,
    )
    xs, ys, normed_one, qkv, kv_all, attn_out, gain_rows, full = front(
        tokens, cotangent, slices, shard, 1
    )
    full = full.reshape(1024, -1)
    ends = [HALF, HALF, 1536, 1024, 1024, 384]
    parts = []
    at = 0
    for n in ends:
        parts.append(full[:, at : at + n])
        at += n
    w_gate, w_up, w_qkv, w_out, w_dn, w_dn_rest = parts
    w_dn = jnp.concatenate([w_dn, w_dn_rest.reshape(384, 1024)], axis=0)
    gain_two = gain_rows[1]
    inputs = xs.astype(F32).reshape(256, WIDTH)
    grad_rows = ys.reshape(256, WIDTH)

    middle = inputs + dot(attn_out, w_out)
    scaled_two, inverse_two = normalize(middle)
    normed_two = (scaled_two * gain_two).astype(BF16)
    gate = dot(normed_two, w_gate)
    upward = dot(normed_two, w_up)
    hidden = (jax.nn.silu(gate) * upward).astype(BF16)
    result_part = dot(hidden, w_dn).reshape(2, 2, 64, WIDTH)
    mid_own = pick(middle.reshape(2, 2, 64, WIDTH).swapaxes(0, 1), core)
    part_own = pick(result_part.swapaxes(0, 1), core)
    part_other = other_core(pick(result_part.swapaxes(0, 1), 1 - core))
    output = (mid_own + (part_own + part_other)).astype(BF16)

    grad_dn = outer_sum(hidden, grad_rows)
    grad_hidden = dot_nt(grad_rows, w_dn)
    squash = jax.nn.sigmoid(gate)
    grad_up = (grad_hidden * jax.nn.silu(gate)).astype(BF16)
    grad_gate = (grad_hidden * upward * (squash + gate * squash * (1.0 - squash))).astype(BF16)
    grad_normed_two = dot_nt(grad_gate, w_gate) + dot_nt(grad_up, w_up)
    grad_normed_two = grad_normed_two + other_core(grad_normed_two)
    grad_middle = grad_rows.astype(F32) + norm_back(
        grad_normed_two * gain_two, scaled_two, inverse_two
    )
    branch_grad = grad_middle.astype(BF16)
    w_out_half = lax.dynamic_slice_in_dim(w_out, core * 512, 512, 0)
    grad_att = dot_nt(branch_grad, w_out_half).astype(BF16)
    branch_half = lax.dynamic_slice_in_dim(branch_grad, core * 512, 512, 1)
    grads = jnp.concatenate(
        [
            outer_sum(normed_two, grad_gate).astype(BF16),
            outer_sum(normed_two, grad_up).astype(BF16),
            outer_sum(attn_out, branch_half).astype(BF16),
            grad_dn[:1024].astype(BF16),
            grad_dn[1024:].astype(BF16).reshape(1024, 384),
        ],
        axis=-1,
    )
    head_grads, grad_normed_one, sums = back(
        qkv, kv_all, normed_one, grad_att, grads, w_qkv, 2
    )
    scaled_one, inverse_one = normalize(tokens.astype(F32))
    grad_inputs = pick(grad_middle.reshape(2, 2, 64, WIDTH).swapaxes(0, 1), core) + norm_back(
        grad_normed_one * gain_rows[0], scaled_one, inverse_one
    )

    wide = 2 * HALF + 512
    rows = sums[:, :wide].reshape(2, 8, wide)
    mine = pick(rows, core)
    theirs = other_core(pick(rows, 1 - core))
    pair = jnp.stack([jnp.where(core == 0, mine, theirs), jnp.where(core == 0, theirs, mine)])
    ffn_part = jnp.stack([from_cores(pair[..., :HALF]), from_cores(pair[..., HALF : 2 * HALF])])
    out_part = jnp.concatenate([pair[0, :, 2 * HALF : wide], pair[1, :, 2 * HALF : wide]], axis=-1)
    head_grads = head_grads.reshape(16, 8, 4, HEAD)
    qkv_part = jnp.stack([head_grads[:, :, i].transpose(1, 0, 2).reshape(8, 1024) for i in (0, 2, 3)])
    attn_part = jnp.concatenate([qkv_part, out_part[None]], axis=0)
    down_part = jnp.concatenate(
        [sums[:, wide : wide + 1024], sums[:, wide + 1024 :].reshape(6, 1024)], axis=0
    )
    gain_part = jnp.stack(
        [
            jnp.sum(attn_low[:3].astype(F32) * qkv_part, axis=(0, 2)),
            jnp.sum(ffn_low.astype(F32) * ffn_part, axis=(0, 2)),
        ]
    ) / gains_low.astype(F32)

    new_attn, second_attn = adam_step(w_attn, m_attn, v_attn, attn_part, 0.06, 0.1)
    new_ffn, second_ffn = adam_step(w_ffn_in, m_ffn_in, v_ffn_in, ffn_part, 0.06, 0.1)
    new_dn, second_dn = adam_step(w_down, m_down, v_down, down_part, 0.04, 0.1)
    new_gn, second_gn = adam_step(gains, m_gains, v_gains, gain_part, 0.4, 0.0)
    return (
        output, grad_inputs, attn_part, ffn_part, down_part, gain_part,
        new_attn, new_ffn, new_dn, new_gn, second_attn, second_ffn, second_dn, second_gn,
    )


def solution(mesh):
    fine = Mesh(mesh.devices.reshape(2, 4, 4, 2, 2), AXES)
    rows3 = P(None, AXES, None)
    rows2 = P(AXES, None)
    cols = P(None, AXES)
    weights = (rows3, rows3, rows2, cols)
    return jax.shard_map(
        body,
        mesh=fine,
        in_specs=(rows3, rows3) + weights * 3,
        out_specs=(rows3, rows3) + weights * 3,
        check_vma=False,
    )
```
